256 devices in a mesh: dom: 32 (over x, y, core), sub: 8 (over z).
Axes of the slice: x: 4, y: 4, z: 8, core: 2. Of those that a mesh axis runs over, the one named last changes fastest.
Arguments:
- points: bfloat16 [524288, 256], P(('dom', 'sub')), may hold values from -60 to 60
- cotangent: bfloat16 [524288, 256], P(('dom', 'sub')), may hold values from -6 to 6
- counts: int32 [32], replicated, may hold values from 8192 to 16384, as said below
- w_in: bfloat16 [256, 512], replicated, may hold values from -0.375 to 0.375
- w_temp: bfloat16 [256, 8], replicated, may hold values from -1 to 1
- slice_weight: bfloat16 [8, 32, 64], replicated, may hold values from -2 to 2
- qkv_weight: float32 [3, 32, 32], replicated, may hold values from -1.5 to 1.5
- w_out: bfloat16 [256, 256], replicated, may hold values from -0.75 to 0.75
- b_out: float32 [256], replicated, may hold values from -3 to 3
Outputs:
- result: bfloat16 [524288, 256], P(('dom', 'sub'))
- grad_points: bfloat16 [524288, 256], P(('dom', 'sub'))
- grad_w_in: float32 [256, 512], replicated
- grad_w_temp: float32 [256, 8], replicated
- grad_slice: float32 [8, 32, 64], replicated
- grad_w_out: float32 [256, 256], replicated
- grad_bias: float32 [256], replicated
- grad_qkv: float32 [3, 32, 32], replicated
The draws below stay inside these ranges and needn't reach their ends.
Inputs may be any that keep to these rules, and one draw needn't show every extreme that they name: `counts`: every count is a multiple of 128 and at least half of 16384 rounded down to tiles of 128; some partition is full in every draw.
All inputs are finite; a program needn't handle non-finite values.
Results may differ from the reference program's by a relative error of at most 0.015.
The reference program's roundings to bfloat16 on the way (of `rounded`, `attended_bf`, `mixed`, `back_mixed`, `grad_numer_bf`, `scaled_bf` and `grad_proj`) count: a program that leaves them out, or rounds other values in their place, can miss the bound.
Values sent between devices are 32-bit elements; how exact they have to be, the bound alone decides.
No kernel may reach another device: no remote copies, remote signals or barrier semaphores. Data moves between devices by JAX's collectives and lax.ppermute only.
A program may use at most 64 MiB of HBM per device.

```python
import jax
import jax.numpy as jnp
from jax import lax

D = 256
HEADS = 8
SLICES = 64
HEAD_DIM = 32
PTS_DEV = 2048
POINTS = 524288
N_DOM = 32
N_SUB = 8


def draw_points(key, part):
    key = jax.random.fold_in(key, 5)
    key_base = jax.random.fold_in(key, 0)
    values = jax.random.normal(key_base, (POINTS, D), jnp.float32)
    return jnp.clip(values, -60.0, 60.0).astype(jnp.bfloat16)


def draw_counts(key, part):
    key = jax.random.fold_in(key, 11)
    key_tiles, key_pick = jax.random.split(key)
    full_tiles = N_SUB * PTS_DEV // 128
    tile_count = jax.random.randint(key_tiles, (N_DOM,), max(1, full_tiles // 2), full_tiles + 1)
    picked = jax.random.randint(key_pick, (), 0, N_DOM)
    tile_count = jnp.where(jnp.arange(N_DOM) == picked, full_tiles, tile_count)
    return (tile_count * 128).astype(jnp.int32)


def block_scale(stream_key, dims, cuts, smallest, largest):
    gain = 1.0
    for axis_at, blocks in cuts:
        steps = jax.random.uniform(jax.random.fold_in(jax.random.fold_in(stream_key, 6), axis_at), (blocks,), jnp.float32, smallest / len(cuts), largest / len(cuts))
        gain = gain * jnp.repeat(jnp.exp(steps), dims[axis_at] // blocks).reshape((-1,) + (1,) * (len(dims) - 1 - axis_at))
    return gain


def bell_draw(stream_key, extent, spread, reach, cuts=(), kind=jnp.bfloat16):
    entries = jax.random.normal(stream_key, extent, jnp.float32) * spread
    if len(cuts) > 0:
        entries = block_scale(stream_key, extent, cuts, -0.22, 0.18) * entries
    return jnp.clip(entries, min=-reach, max=reach).astype(kind)


def setup_inputs(seed: int = 0) -> dict:
    key_of = jax.random.split(jax.random.key(seed), 10)
    return {
        "points": draw_points(jax.random.fold_in(key_of[9], 71), 0),
        "cotangent": bell_draw(key_of[1], (POINTS, D), 1.0, 6.0, ((0, 256),)),
        "counts": draw_counts(jax.random.fold_in(key_of[9], 71), 0),
        "w_in": bell_draw(key_of[3], (D, 2 * D), D ** -0.5, 0.375),
        "w_temp": bell_draw(key_of[4], (D, HEADS), (D / 8) ** -0.5, 1.0),
        "slice_weight": bell_draw(key_of[5], (HEADS, HEAD_DIM, SLICES), (HEAD_DIM / 4) ** -0.5, 2.0),
        "qkv_weight": bell_draw(key_of[6], (3, HEAD_DIM, HEAD_DIM), (HEAD_DIM / 2) ** -0.5, 1.5, (), jnp.float32),
        "w_out": bell_draw(key_of[7], (D, D), (D / 4) ** -0.5, 0.75),
        "b_out": bell_draw(key_of[8], (D,), 0.5, 3.0, (), jnp.float32),
    }


EPSILON = 1e-05

def forward_block(points, inside, w_in, w_temp, slice_weight):
    row_count = points.shape[0]
    model_width = points.shape[1]
    head_count = slice_weight.shape[0]
    head_width = model_width // head_count
    projected = jnp.dot(points, w_in, preferred_element_type=jnp.float32)
    feature_x = projected[:, :model_width].astype(jnp.bfloat16).reshape(row_count, head_count, head_width)
    feature_f = projected[:, model_width:].astype(jnp.bfloat16).reshape(row_count, head_count, head_width)
    sigmoid_gate = jax.nn.sigmoid(jnp.dot(points, w_temp, preferred_element_type=jnp.float32))
    temper = 0.5 + 1.5 * sigmoid_gate
    raw_score = jnp.einsum('rhe,hem->rhm', feature_x.astype(jnp.float32), slice_weight.astype(jnp.float32))
    logits = raw_score / temper[:, :, None]
    shares = jax.nn.softmax(logits, axis=-1)
    masked = shares * inside[:, None, None]
    rounded = masked.astype(jnp.bfloat16)
    return (feature_x, feature_f, sigmoid_gate, temper, logits, shares, masked, rounded)

def attend_slices(tokens, qkv_weight):
    high = lax.Precision.HIGHEST
    query = jnp.einsum('hme,ef->hmf', tokens, qkv_weight[0], precision=high)
    keys_all = jnp.einsum('hme,ef->hmf', tokens, qkv_weight[1], precision=high)
    values = jnp.einsum('hme,ef->hmf', tokens, qkv_weight[2], precision=high)
    scores = jnp.einsum('hmf,hnf->hmn', query, keys_all, precision=high) * tokens.shape[-1] ** (-0.5)
    weights = jax.nn.softmax(scores, axis=-1)
    return jnp.einsum('hmn,hnf->hmf', weights, values, precision=high)

def output_block(rounded, attended_bf, inside, cotangent, w_out, b_out):
    row_count = rounded.shape[0]
    model_width = w_out.shape[0]
    mixed = jnp.einsum('rhm,hme->rhe', rounded.astype(jnp.float32), attended_bf.astype(jnp.float32))
    mixed_bf = mixed.astype(jnp.bfloat16).reshape(row_count, model_width)
    result = ((jnp.dot(mixed_bf, w_out, preferred_element_type=jnp.float32) + b_out) * inside[:, None]).astype(jnp.bfloat16)
    grad_w_out = jnp.einsum('rd,rc->dc', mixed_bf.astype(jnp.float32), cotangent.astype(jnp.float32))
    grad_bias = lax.optimization_barrier(jnp.sum(cotangent.astype(jnp.float32) * inside[:, None], axis=0))
    back_full = jnp.einsum('rc,dc->rd', cotangent.astype(jnp.float32), w_out.astype(jnp.float32))
    back_mixed = (back_full.reshape(row_count, attended_bf.shape[0], attended_bf.shape[2]) * inside[:, None, None]).astype(jnp.bfloat16)
    grad_att = jnp.einsum('rhm,rhe->hme', rounded.astype(jnp.float32), back_mixed.astype(jnp.float32))
    grad_shares = jnp.einsum('rhe,hme->rhm', back_mixed.astype(jnp.float32), attended_bf.astype(jnp.float32))
    return (result, grad_w_out, grad_bias, grad_att, grad_shares)

def input_block(points, inside, parts, grad_shares, grad_numer_bf, grad_totals, w_in, w_temp, slice_weight):
    feature_x, feature_f, sigmoid_gate, temper, logits, shares, masked, rounded = parts
    row_count = points.shape[0]
    model_width = points.shape[1]
    total_share = grad_shares + grad_totals[None] + jnp.einsum('rhe,hme->rhm', feature_f.astype(jnp.float32), grad_numer_bf.astype(jnp.float32))
    grad_logits = inside[:, None, None] * shares * (total_share - lax.optimization_barrier(jnp.sum(shares * total_share, axis=-1, keepdims=True)))
    scaled = grad_logits / temper[:, :, None]
    scaled_bf = scaled.astype(jnp.bfloat16)
    grad_fx_x = jnp.einsum('rhm,hem->rhe', scaled_bf.astype(jnp.float32), slice_weight.astype(jnp.float32))
    grad_slice = jnp.einsum('rhe,rhm->hem', feature_x.astype(jnp.float32), scaled_bf.astype(jnp.float32))
    grad_temper = -lax.optimization_barrier(jnp.sum(scaled * logits, axis=-1))
    grad_temp_pre = (grad_temper * 1.5 * sigmoid_gate * (1.0 - sigmoid_gate)).astype(jnp.bfloat16)
    grad_fx_f = jnp.einsum('rhm,hme->rhe', rounded.astype(jnp.float32), grad_numer_bf.astype(jnp.float32))
    grad_proj = jnp.concatenate([grad_fx_x.reshape(row_count, model_width), grad_fx_f.reshape(row_count, model_width)], axis=1).astype(jnp.bfloat16)
    grad_w_in = jnp.einsum('rd,rk->dk', points.astype(jnp.float32), grad_proj.astype(jnp.float32))
    grad_w_temp = jnp.einsum('rd,rk->dk', points.astype(jnp.float32), grad_temp_pre.astype(jnp.float32))
    grad_points = (jnp.einsum('rk,dk->rd', grad_proj.astype(jnp.float32), w_in.astype(jnp.float32)) + jnp.einsum('rk,dk->rd', grad_temp_pre.astype(jnp.float32), w_temp.astype(jnp.float32))).astype(jnp.bfloat16)
    return (grad_points, grad_w_in, grad_w_temp, grad_slice)

def reference(points, cotangent, counts, w_in, w_temp, slice_weight, qkv_weight, w_out, b_out):
    part_rows = N_SUB * PTS_DEV
    point_blocks = points.reshape(N_DOM, part_rows, D)
    cot_blocks = cotangent.reshape(N_DOM, part_rows, D)

    def inside_of(count):
        return (jnp.arange(part_rows, dtype=jnp.int32) < count).astype(jnp.float32)

    def first_pass(carry, item):
        block, count = item
        parts = forward_block(block, inside_of(count), w_in, w_temp, slice_weight)
        numer = jnp.einsum('rhm,rhe->hme', parts[7].astype(jnp.float32), parts[1].astype(jnp.float32))
        return ((carry[0] + lax.optimization_barrier(jnp.sum(parts[6], axis=0)), carry[1] + numer), None)
    start_one = (jnp.zeros((HEADS, SLICES), jnp.float32), jnp.zeros((HEADS, SLICES, HEAD_DIM), jnp.float32))
    (totals, numer), unused = lax.scan(first_pass, start_one, (point_blocks, counts))
    tokens = numer / (totals + EPSILON)[:, :, None]
    attended, pullback = jax.vjp(attend_slices, tokens, qkv_weight)
    attended_bf = attended.astype(jnp.bfloat16)

    def second_pass(carry, item):
        block, cot_block, count = item
        inside = inside_of(count)
        parts = forward_block(block, inside, w_in, w_temp, slice_weight)
        result, grad_w_out, grad_bias, grad_att, grad_shares = output_block(parts[7], attended_bf, inside, cot_block, w_out, b_out)
        return ((carry[0] + grad_w_out, carry[1] + grad_bias, carry[2] + grad_att), result)
    start_two = (jnp.zeros((D, D), jnp.float32), jnp.zeros((D,), jnp.float32), jnp.zeros((HEADS, SLICES, HEAD_DIM), jnp.float32))
    (grad_w_out, grad_bias, grad_att), result = lax.scan(second_pass, start_two, (point_blocks, cot_blocks, counts))
    grad_tokens, grad_qkv = pullback(grad_att)
    grad_numer = grad_tokens / (totals + EPSILON)[:, :, None]
    grad_totals = -lax.optimization_barrier(jnp.sum(grad_tokens * tokens, axis=-1)) / (totals + EPSILON)
    grad_numer_bf = grad_numer.astype(jnp.bfloat16)

    def third_pass(carry, item):
        block, cot_block, count = item
        inside = inside_of(count)
        parts = forward_block(block, inside, w_in, w_temp, slice_weight)
        unused_out = output_block(parts[7], attended_bf, inside, cot_block, w_out, b_out)
        grad_points, grad_w_in, grad_w_temp, grad_slice = input_block(block, inside, parts, unused_out[4], grad_numer_bf, grad_totals, w_in, w_temp, slice_weight)
        return ((carry[0] + grad_w_in, carry[1] + grad_w_temp, carry[2] + grad_slice), grad_points)
    start_three = (jnp.zeros((D, 2 * D), jnp.float32), jnp.zeros((D, HEADS), jnp.float32), jnp.zeros((HEADS, HEAD_DIM, SLICES), jnp.float32))
    (grad_w_in, grad_w_temp, grad_slice), grad_points = lax.scan(third_pass, start_three, (point_blocks, cot_blocks, counts))
    return (result.reshape(POINTS, D), grad_points.reshape(POINTS, D), grad_w_in, grad_w_temp, grad_slice, grad_w_out, grad_bias, grad_qkv)
```

```python
import jax
import jax.numpy as jnp
from jax import lax
from jax.experimental import pallas as pl
from jax.experimental.pallas import tpu as pltpu
from jax.sharding import Mesh, PartitionSpec as P

EPSILON = 1e-05
F32 = jnp.float32
BF16 = jnp.bfloat16
HIGH = lax.Precision.HIGHEST

D = 256
HEADS = 8
SLICES = 64
WIDTH = 32
ROWS = 2048
SUBS = 8
CHUNK = 256
HALF = 896
VMEM_LIMIT = 48 * 1024 * 1024
SMALL_LIMIT = 16 * 1024 * 1024


def nn(a, b, precision=None):
    return lax.dot_general(
        a, b, (((1,), (0,)), ((), ())), preferred_element_type=F32, precision=precision
    )


def nt(a, b, precision=None):
    return lax.dot_general(
        a, b, (((1,), (1,)), ((), ())), preferred_element_type=F32, precision=precision
    )


def tn(a, b, precision=None):
    return lax.dot_general(
        a, b, (((0,), (0,)), ((), ())), preferred_element_type=F32, precision=precision
    )


def lane_ids(shape):
    return lax.broadcasted_iota(jnp.int32, shape, 1)


def device_place():
    x, y = lax.axis_index("x"), lax.axis_index("y")
    core, sub = lax.axis_index("core"), lax.axis_index("sub")
    return (x * 4 + y) * 2 + core, sub, core


def live_rows(counts_ref):
    dom, sub, _ = device_place()
    return counts_ref[dom] - sub * ROWS


def in_hbm(*arrays):
    return [pltpu.with_memory_space_constraint(a, pltpu.HBM) for a in arrays]


def inside_row(limit, step):
    place = step * CHUNK + lane_ids((1, CHUNK))
    return jnp.where(place < limit, 1.0, 0.0).astype(F32)


def forward_kernel(
    counts_ref,
    points_ref,
    cot_ref,
    w_in_ref,
    w_temp_ref,
    sw_ref,
    w_out_ref,
    packed_ref,
    bias_ref,
    fx_ref,
    fb_ref,
    shares_ref,
    gate_ref,
    sw_rows_ref,
    sw_cols_ref,
    w_in_t,
    w_temp_t,
    sw_pad,
    acc,
    tot,
):
    step = pl.program_id(0)
    limit = live_rows(counts_ref)

    @pl.when(step == 0)
    def _():
        w_in_t[...] = w_in_ref[...].astype(F32).T.astype(BF16)
        w_temp_t[...] = w_temp_ref[...]
        for group in range(2):
            sw_pad[...] = jnp.zeros_like(sw_pad)
            for j in range(4):
                sw_pad[32 * j : 32 * j + 32, 64 * j : 64 * j + 64] = sw_ref[
                    4 * group + j
                ].astype(F32)
            rows = sw_pad[...]
            sw_rows_ref[group] = rows.astype(BF16)
            sw_cols_ref[group] = rows.T.astype(BF16)
        acc[...] = jnp.zeros_like(acc)
        tot[...] = jnp.zeros_like(tot)
        bias_ref[...] = jnp.zeros_like(bias_ref)

    inside = inside_row(limit, step)
    points = points_ref[...]
    cot = cot_ref[...]
    gate = jax.nn.sigmoid(nt(w_temp_t[...], points))
    gate_ref[...] = gate
    inv_temper = 1.0 / (0.5 + 1.5 * gate)
    proj_x = nt(w_in_t[0:D, :], points).astype(BF16)
    fx_ref[...] = proj_x
    proj_f = nt(w_in_t[D : 2 * D, :], points).astype(BF16)
    back = (nt(w_out_ref[...], cot) * inside).astype(BF16)
    for h in range(HEADS):
        fb_ref[64 * h : 64 * h + 32, :] = back[32 * h : 32 * h + 32]
        fb_ref[64 * h + 32 : 64 * h + 64, :] = proj_f[32 * h : 32 * h + 32]
    bias_ref[...] += nn(jnp.broadcast_to(inside, (8, CHUNK)).astype(BF16), cot)
    for group in range(2):
        raw = nn(sw_cols_ref[group], proj_x[128 * group : 128 * group + 128])
        pieces = []
        for j in range(4):
            h = 4 * group + j
            logits = raw[64 * j : 64 * j + 64] * inv_temper[h : h + 1]
            top = jnp.max(logits, axis=0, keepdims=True)
            ex = jnp.exp(logits - top)
            shares = ex * (1.0 / jnp.sum(ex, axis=0, keepdims=True))
            shares_ref[64 * h : 64 * h + 64, :] = shares
            masked = shares * inside
            folded = masked[:, 0:128]
            for k in range(1, CHUNK // 128):
                folded = folded + masked[:, 128 * k : 128 * k + 128]
            tot[64 * h : 64 * h + 64, :] += folded
            pieces.append(masked.astype(BF16))
        rounded = jnp.concatenate(pieces, axis=0)
        acc[group] += nt(rounded, fb_ref[256 * group : 256 * group + 256, :])

    @pl.when(step == pl.num_programs(0) - 1)
    def _():
        low = lane_ids((32, 128)) < 64
        totals = nt(jnp.ones((8, 128), F32), tot[...], HIGH)
        for h in range(HEADS):
            group, j = divmod(h, 4)
            lanes = 128 * (j // 2)
            block = acc[group, 64 * j : 64 * j + 64, lanes : lanes + 128]
            upper, lower = block[0:32], block[32:64]
            row = totals[:, 128 * (h // 2) : 128 * (h // 2) + 128]
            if j % 2 == 0:
                both = jnp.where(low, upper, pltpu.roll(lower, 64, 1))
            else:
                both = jnp.where(low, pltpu.roll(upper, 64, 1), lower)
                row = pltpu.roll(row, 64, 1)
            packed_ref[h, 0:32, :] = both
            packed_ref[h, 32:40, :] = row


def forward_call(counts, points, cotangent, w_in, w_temp, slice_weight, w_out):
    whole = pl.BlockSpec(memory_space=pltpu.VMEM)
    row_block = pl.BlockSpec((CHUNK, D), lambda i: (i, 0))

    def lane_block(rows):
        return pl.BlockSpec((rows, CHUNK), lambda i: (0, i))

    def fixed(shape):
        return pl.BlockSpec(shape, lambda i: (0,) * len(shape))

    return pl.pallas_call(
        forward_kernel,
        grid=(ROWS // CHUNK,),
        in_specs=[
            pl.BlockSpec(memory_space=pltpu.SMEM),
            row_block,
            row_block,
            fixed((D, 2 * D)),
            fixed((HEADS, D)),
            fixed((HEADS, WIDTH, SLICES)),
            fixed((D, D)),
        ],
        out_specs=[
            fixed((HEADS, 40, 128)),
            fixed((8, D)),
            lane_block(D),
            lane_block(2 * D),
            lane_block(2 * D),
            lane_block(HEADS),
            fixed((2, 128, 256)),
            fixed((2, 256, 128)),
        ],
        out_shape=[
            jax.ShapeDtypeStruct((HEADS, 40, 128), F32),
            jax.ShapeDtypeStruct((8, D), F32),
            jax.ShapeDtypeStruct((D, ROWS), BF16),
            jax.ShapeDtypeStruct((2 * D, ROWS), BF16),
            jax.ShapeDtypeStruct((2 * D, ROWS), F32),
            jax.ShapeDtypeStruct((HEADS, ROWS), F32),
            jax.ShapeDtypeStruct((2, 128, 256), BF16),
            jax.ShapeDtypeStruct((2, 256, 128), BF16),
        ],
        scratch_shapes=[
            pltpu.VMEM((2 * D, D), BF16),
            pltpu.VMEM((HEADS, D), BF16),
            pltpu.VMEM((128, 256), F32),
            pltpu.VMEM((2, 256, 256), F32),
            pltpu.VMEM((2 * D, 128), F32),
        ],
        compiler_params=pltpu.CompilerParams(
            dimension_semantics=("arbitrary",), vmem_limit_bytes=VMEM_LIMIT
        ),
        name="forward",
    )(counts, *in_hbm(points, cotangent, w_in, w_temp.T, slice_weight, w_out))


def attention_kernel(parts_ref, qkv_ref, out_ref, grad_qkv_ref):
    summed = parts_ref[0]
    for k in range(1, parts_ref.shape[0]):
        summed = summed + parts_ref[k]
    pairs = jnp.concatenate([summed[0:32], pltpu.roll(summed[0:32], 64, 1)], axis=0)
    grad_att = pairs[:, 0:WIDTH]
    numer = pltpu.roll(pairs, 96, 1)[:, 0:WIDTH]
    totals = jnp.concatenate([summed[32:40]] * 16, axis=0).T[0:SLICES, 0:1]
    inv = 1.0 / (totals + EPSILON)
    tokens = numer * inv
    w_q, w_k, w_v = qkv_ref[0], qkv_ref[1], qkv_ref[2]
    scale = WIDTH**-0.5
    query = nn(tokens, w_q, HIGH)
    keys = nn(tokens, w_k, HIGH)
    values = nn(tokens, w_v, HIGH)
    scores = nt(query, keys, HIGH) * scale
    ex = jnp.exp(scores - jnp.max(scores, axis=1, keepdims=True))
    weights = ex / jnp.sum(ex, axis=1, keepdims=True)
    attended = nn(weights, values, HIGH)
    grad_values = tn(weights, grad_att, HIGH)
    grad_weights = nt(grad_att, values, HIGH)
    inner = jnp.sum(weights * grad_weights, axis=1, keepdims=True)
    grad_scores = weights * (grad_weights - inner) * scale
    grad_query = nn(grad_scores, keys, HIGH)
    grad_keys = tn(grad_scores, query, HIGH)
    grad_tokens = (
        nt(grad_query, w_q, HIGH) + nt(grad_keys, w_k, HIGH) + nt(grad_values, w_v, HIGH)
    )
    grad_qkv_ref[...] = jnp.zeros_like(grad_qkv_ref)
    for i, grad in enumerate((grad_query, grad_keys, grad_values)):
        grad_qkv_ref[:, WIDTH * i : WIDTH * i + WIDTH] = tn(tokens, grad, HIGH) * (1.0 / 32)
    grad_numer = grad_tokens * inv
    grad_totals = -jnp.sum(grad_tokens * tokens, axis=1, keepdims=True) * inv
    grad_row = jnp.broadcast_to(grad_totals, (SLICES, 128)).T[0:8]
    for k in range(out_ref.shape[0]):
        out_ref[k, 0:32, 0:32] = attended[0:32]
        out_ref[k, 0:32, 32:64] = grad_numer[0:32]
        out_ref[k, 0:32, 64:96] = attended[32:64]
        out_ref[k, 0:32, 96:128] = grad_numer[32:64]
        out_ref[k, 32:40, 0:64] = grad_row
        out_ref[k, 32:40, 64:128] = grad_row


def attention_call(parts, qkv_weight):
    whole = pl.BlockSpec(memory_space=pltpu.VMEM)
    return pl.pallas_call(
        attention_kernel,
        in_specs=[whole, whole],
        out_specs=[whole, whole],
        out_shape=[
            jax.ShapeDtypeStruct((SUBS, 40, 128), F32),
            jax.ShapeDtypeStruct((WIDTH, 128), F32),
        ],
        compiler_params=pltpu.CompilerParams(vmem_limit_bytes=SMALL_LIMIT),
        name="slice_attention",
    )(parts, qkv_weight)


def backward_kernel(
    counts_ref,
    points_ref,
    cot_ref,
    fx_ref,
    fb_ref,
    shares_ref,
    gate_ref,
    sw_rows_ref,
    sw_cols_ref,
    heads_ref,
    bias_ref,
    grad_qkv_ref,
    w_in_ref,
    w_temp_ref,
    w_out_ref,
    b_out_ref,
    result_ref,
    grad_points_ref,
    mine_ref,
    theirs_ref,
    token_pad,
    token_cols,
    token_rows,
    grad_tot,
    w_out_t,
    temp_pad,
    mixed_ref,
    proj_ref,
    acc_slice,
    acc_out,
    acc_in,
    acc_temp,
):
    step = pl.program_id(0)
    limit = live_rows(counts_ref)

    @pl.when(step == 0)
    def _():
        w_out_t[...] = w_out_ref[...].astype(F32).T.astype(BF16)
        temp_pad[...] = jnp.concatenate(
            [w_temp_ref[...].astype(F32), jnp.zeros((120, D), F32)], axis=0
        ).T.astype(BF16)
        rows = [heads_ref[h, 32:33, :] for h in range(HEADS)]
        square = jnp.concatenate(rows * 16, axis=0).T
        low = lane_ids((64, 128)) < 64
        for group in range(2):
            token_pad[...] = jnp.zeros_like(token_pad)
            for j in range(4):
                h = 4 * group + j
                both = heads_ref[h, 0:32, :]
                turned = pltpu.roll(both, 64, 1)
                lanes = 128 * (j // 2)
                if j % 2 == 0:
                    block = jnp.concatenate([both, turned], axis=0)
                    block = jnp.where(low, block, 0.0)
                else:
                    block = jnp.concatenate([turned, both], axis=0)
                    block = jnp.where(low, 0.0, block)
                token_pad[64 * j : 64 * j + 64, lanes : lanes + 128] = block
                grad_tot[64 * h : 64 * h + 64, :] = jnp.broadcast_to(
                    square[0:64, h : h + 1], (64, 128)
                )
            token_cols[group] = token_pad[...].astype(BF16)
            token_rows[group] = token_pad[...].T.astype(BF16)
        acc_slice[...] = jnp.zeros_like(acc_slice)
        acc_out[...] = jnp.zeros_like(acc_out)
        acc_in[...] = jnp.zeros_like(acc_in)
        acc_temp[...] = jnp.zeros_like(acc_temp)

    inside = inside_row(limit, step)
    points = points_ref[...]
    cot = cot_ref[...]
    gate = gate_ref[...]
    inv_temper = 1.0 / (0.5 + 1.5 * gate)
    scale_temp = -1.5 * gate * (1.0 - gate) * inv_temper
    temp_rows = []
    for group in range(2):
        fx = fx_ref[128 * group : 128 * group + 128, :]
        raw = nn(sw_cols_ref[group], fx)
        total = nn(token_cols[group], fb_ref[256 * group : 256 * group + 256, :])
        scaled_parts = []
        rounded_parts = []
        for j in range(4):
            h = 4 * group + j
            shares = shares_ref[64 * h : 64 * h + 64, :]
            gt = grad_tot[64 * h : 64 * h + 64, :]
            share_grad = total[64 * j : 64 * j + 64] + jnp.concatenate(
                [gt] * (CHUNK // 128), axis=1
            )
            weighted = shares * share_grad
            inner = jnp.sum(weighted, axis=0, keepdims=True)
            factor = inside * inv_temper[h : h + 1]
            scaled = shares * (share_grad - inner) * factor
            temp_rows.append(
                jnp.sum(scaled * raw[64 * j : 64 * j + 64], axis=0, keepdims=True)
                * scale_temp[h : h + 1]
            )
            scaled_parts.append(scaled.astype(BF16))
            rounded_parts.append((shares * inside).astype(BF16))
        scaled_bf = jnp.concatenate(scaled_parts, axis=0)
        rounded = jnp.concatenate(rounded_parts, axis=0)
        acc_slice[group] += nt(fx, scaled_bf)
        proj_ref[128 * group : 128 * group + 128, :] = nn(sw_rows_ref[group], scaled_bf).astype(
            BF16
        )
        pair = nn(token_rows[group], rounded).astype(BF16)
        for j in range(4):
            h = 4 * group + j
            mixed_ref[32 * h : 32 * h + 32, :] = pair[64 * j : 64 * j + 32]
            proj_ref[D + 32 * h : D + 32 * h + 32, :] = pair[64 * j + 32 : 64 * j + 64]
    temp_grad = jnp.concatenate(
        temp_rows + [jnp.zeros((8, CHUNK), F32)], axis=0
    ).astype(BF16)
    mixed = mixed_ref[...]
    proj = proj_ref[...]
    out = nn(w_out_t[...], mixed).T
    column = lax.broadcasted_iota(jnp.int32, (CHUNK, 1), 0) + step * CHUNK
    live = jnp.where(column < limit, 1.0, 0.0)
    result_ref[...] = ((out + b_out_ref[...]) * live).astype(BF16)
    acc_out[...] += nn(mixed, cot)
    acc_in[...] += nn(proj, points)
    acc_temp[...] += nn(temp_grad, points)
    grad = nn(w_in_ref[...], proj) + nn(temp_pad[...][:, 0:16], temp_grad)
    grad_points_ref[...] = grad.T.astype(BF16)

    @pl.when(step == pl.num_programs(0) - 1)
    def _():
        low = lane_ids((32, 128)) < 64

        def write_first(ref):
            for k in range(3):
                ref[256 * k : 256 * k + 256, :] = acc_in[128 * k : 128 * k + 128, :].T
            for k in range(4):
                group, pair = divmod(k, 2)
                block = acc_slice[group, 64 * pair : 64 * pair + 64, 128 * pair : 128 * pair + 128]
                ref[768 + 32 * k : 800 + 32 * k, :] = jnp.where(low, block[0:32], block[32:64])

        def write_second(ref):
            ref[0:256, :] = acc_in[384:512, :].T
            ref[256:512, :] = acc_out[:, 0:128]
            ref[512:768, :] = acc_out[:, 128:256]
            ref[768:776, :] = acc_temp[0:8, 0:128]
            ref[776:784, :] = acc_temp[0:8, 128:256]
            ref[784:792, :] = bias_ref[:, 0:128]
            ref[792:800, :] = bias_ref[:, 128:256]
            ref[800:832, :] = grad_qkv_ref[...]
            ref[832:HALF, :] = jnp.zeros((HALF - 832, 128), F32)

        core = device_place()[2]

        @pl.when(core == 0)
        def _():
            write_first(mine_ref)
            write_second(theirs_ref)

        @pl.when(core != 0)
        def _():
            write_first(theirs_ref)
            write_second(mine_ref)


def backward_call(counts, points, cotangent, stash, heads, bias, grad_qkv, w_in, w_temp, w_out, b_out):
    fx, fb, shares, gate, sw_rows, sw_cols = stash
    row_block = pl.BlockSpec((CHUNK, D), lambda i: (i, 0))

    def lane_block(rows):
        return pl.BlockSpec((rows, CHUNK), lambda i: (0, i))

    def fixed(shape):
        return pl.BlockSpec(shape, lambda i: (0,) * len(shape))

    return pl.pallas_call(
        backward_kernel,
        grid=(ROWS // CHUNK,),
        in_specs=[
            pl.BlockSpec(memory_space=pltpu.SMEM),
            row_block,
            row_block,
            lane_block(D),
            lane_block(2 * D),
            lane_block(2 * D),
            lane_block(HEADS),
            fixed((2, 128, 256)),
            fixed((2, 256, 128)),
            fixed((HEADS, 40, 128)),
            fixed((8, D)),
            fixed((WIDTH, 128)),
            fixed((D, 2 * D)),
            fixed((HEADS, D)),
            fixed((D, D)),
            fixed((1, D)),
        ],
        out_specs=[row_block, row_block, fixed((HALF, 128)), fixed((HALF, 128))],
        out_shape=[
            jax.ShapeDtypeStruct((ROWS, D), BF16),
            jax.ShapeDtypeStruct((ROWS, D), BF16),
            jax.ShapeDtypeStruct((HALF, 128), F32),
            jax.ShapeDtypeStruct((HALF, 128), F32),
        ],
        scratch_shapes=[
            pltpu.VMEM((256, 256), F32),
            pltpu.VMEM((2, 256, 256), BF16),
            pltpu.VMEM((2, 256, 256), BF16),
            pltpu.VMEM((2 * D, 128), F32),
            pltpu.VMEM((D, D), BF16),
            pltpu.VMEM((D, 128), BF16),
            pltpu.VMEM((D, CHUNK), BF16),
            pltpu.VMEM((2 * D, CHUNK), BF16),
            pltpu.VMEM((2, 128, 256), F32),
            pltpu.VMEM((D, D), F32),
            pltpu.VMEM((2 * D, D), F32),
            pltpu.VMEM((16, D), F32),
        ],
        compiler_params=pltpu.CompilerParams(
            dimension_semantics=("arbitrary",), vmem_limit_bytes=VMEM_LIMIT
        ),
        name="backward",
    )(
        counts,
        points,
        cotangent,
        fx,
        fb,
        shares,
        gate,
        *in_hbm(sw_rows, sw_cols),
        heads,
        bias,
        *in_hbm(grad_qkv, w_in, w_temp.T, w_out, b_out.reshape(1, D)),
    )


def sum_spread(parts, copies):
    summed = jnp.sum(parts, axis=0)
    return jnp.broadcast_to(summed[None], (copies,) + summed.shape)


def unpack_kernel(
    mine_ref,
    theirs_ref,
    grad_in_ref,
    grad_temp_ref,
    grad_slice_ref,
    grad_out_ref,
    grad_bias_ref,
    grad_qkv_ref,
):
    def unpack(first, second):
        for k in range(3):
            grad_in_ref[:, 128 * k : 128 * k + 128] = first[256 * k : 256 * k + 256, :]
        grad_in_ref[:, 384:512] = second[0:256, :]
        for k in range(4):
            block = first[768 + 32 * k : 800 + 32 * k, :]
            grad_slice_ref[2 * k] = block[:, 0:64]
            grad_slice_ref[2 * k + 1] = pltpu.roll(block, 64, 1)[:, 0:64]
        grad_out_ref[:, 0:128] = second[256:512, :]
        grad_out_ref[:, 128:256] = second[512:768, :]
        for k in range(2):
            rows = second[768 + 8 * k : 776 + 8 * k, :]
            grad_temp_ref[:, 128 * k : 128 * k + 128] = rows
            grad_bias_ref[0:1, 128 * k : 128 * k + 128] = second[784 + 8 * k : 785 + 8 * k, :]
        qkv = second[800:832, :]
        grad_qkv_ref[0] = qkv[:, 0:32]
        grad_qkv_ref[1] = pltpu.roll(qkv, 96, 1)[:, 0:32]
        grad_qkv_ref[2] = pltpu.roll(qkv, 64, 1)[:, 0:32]

    core = device_place()[2]

    @pl.when(core == 0)
    def _():
        unpack(mine_ref, theirs_ref)

    @pl.when(core != 0)
    def _():
        unpack(theirs_ref, mine_ref)


def unpack_call(mine, theirs):
    whole = pl.BlockSpec(memory_space=pltpu.VMEM)
    return pl.pallas_call(
        unpack_kernel,
        in_specs=[whole, whole],
        out_specs=[whole] * 6,
        out_shape=[
            jax.ShapeDtypeStruct((D, 2 * D), F32),
            jax.ShapeDtypeStruct((HEADS, D), F32),
            jax.ShapeDtypeStruct((HEADS, WIDTH, SLICES), F32),
            jax.ShapeDtypeStruct((D, D), F32),
            jax.ShapeDtypeStruct((1, D), F32),
            jax.ShapeDtypeStruct((3, WIDTH, WIDTH), F32),
        ],
        compiler_params=pltpu.CompilerParams(vmem_limit_bytes=SMALL_LIMIT),
        name="unpack",
    )(mine, theirs)


def swap_cores(values):
    return lax.ppermute(values, "core", [(0, 1), (1, 0)])


def spread_over(values, axes):
    return lax.all_to_all(values, axes, 0, 0)


def per_device(points, cotangent, counts, w_in, w_temp, slice_weight, qkv_weight, w_out, b_out):
    packed, bias, *stash = forward_call(
        counts, points, cotangent, w_in, w_temp, slice_weight, w_out
    )
    packed = packed + swap_cores(packed)
    parts = sum_spread(spread_over(packed, "sub"), 16)
    parts = spread_over(parts, ("x", "y"))
    heads, grad_qkv = attention_call(parts, qkv_weight)
    heads = spread_over(heads, "sub")
    result, grad_points, mine, theirs = backward_call(
        counts, points, cotangent, stash, heads, bias, grad_qkv, w_in, w_temp, w_out, b_out
    )
    mine = (mine + swap_cores(theirs)).reshape(16, HALF // 16, 128)
    mine = sum_spread(spread_over(mine, ("x", "y")), SUBS)
    mine = sum_spread(spread_over(mine, "sub"), 16)
    mine = spread_over(mine, ("x", "y")).reshape(HALF, 128)
    grad_w_in, grad_w_temp, grad_slice, grad_w_out, grad_bias, grad_qkv = unpack_call(mine, swap_cores(mine))
    return (
        result,
        grad_points,
        grad_w_in,
        grad_w_temp.T,
        grad_slice,
        grad_w_out,
        grad_bias.reshape(D),
        grad_qkv,
    )


def solution(mesh):
    fine = Mesh(mesh.devices.reshape(4, 4, 2, 8), ("x", "y", "core", "sub"))
    rows = P(("x", "y", "core", "sub"), None)
    return jax.shard_map(
        per_device,
        mesh=fine,
        in_specs=(rows, rows) + (P(),) * 7,
        out_specs=(rows, rows) + (P(),) * 6,
        check_vma=False,
    )
```

```python
import jax
import jax.numpy as jnp
from jax import lax
from jax.experimental import pallas as pl
from jax.experimental.pallas import tpu as pltpu
from jax.sharding import Mesh, PartitionSpec as P

EPSILON = 1e-05
F32 = jnp.float32
BF16 = jnp.bfloat16
HIGH = lax.Precision.HIGHEST

D = 256
HEADS = 8
SLICES = 64
WIDTH = 32
ROWS = 2048
SUBS = 8
CHUNK = 2048
HALF = 896
STEPS = ROWS // CHUNK
VMEM_LIMIT = 40 * 1024 * 1024
SMALL_LIMIT = 16 * 1024 * 1024


def nn(a, b, precision=None):
    return lax.dot_general(
        a, b, (((1,), (0,)), ((), ())), preferred_element_type=F32, precision=precision
    )


def nt(a, b, precision=None):
    return lax.dot_general(
        a, b, (((1,), (1,)), ((), ())), preferred_element_type=F32, precision=precision
    )


def tn(a, b, precision=None):
    return lax.dot_general(
        a, b, (((0,), (0,)), ((), ())), preferred_element_type=F32, precision=precision
    )


def lane_ids(shape):
    return lax.broadcasted_iota(jnp.int32, shape, 1)


def device_place():
    x, y = lax.axis_index("x"), lax.axis_index("y")
    core, sub = lax.axis_index("core"), lax.axis_index("sub")
    return (x * 4 + y) * 2 + core, sub, core


def live_rows(counts_ref):
    dom, sub, _ = device_place()
    return counts_ref[dom] - sub * ROWS


def in_hbm(*arrays):
    return [pltpu.with_memory_space_constraint(a, pltpu.HBM) for a in arrays]


def inside_row(limit, step):
    place = step * CHUNK + lane_ids((1, CHUNK))
    return jnp.where(place < limit, 1.0, 0.0).astype(F32)


def stash_copies(step, group, outside, inner, sems, outward):
    rows = pl.ds(256 * group, 256)
    lanes = pl.ds(step * CHUNK, CHUNK)
    if not isinstance(step, int):
        lanes = pl.ds(pl.multiple_of(step * CHUNK, CHUNK), CHUNK)
    copies = []
    for k, (far, near) in enumerate(zip(outside, inner)):
        far, near = far.at[rows, lanes], near.at[rows, lanes]
        ends = (near, far) if outward else (far, near)
        copies.append(pltpu.make_async_copy(*ends, sems.at[step, group, k]))
    return copies


def forward_kernel(
    counts_ref,
    points_ref,
    cot_ref,
    w_in_ref,
    w_temp_ref,
    sw_ref,
    w_out_ref,
    packed_ref,
    fx_ref,
    gate_ref,
    fb_hbm,
    shares_hbm,
    raw_hbm,
    fb_ref,
    shares_ref,
    raw_ref,
    sw_cols_ref,
    w_all_t,
    sw_pad,
    acc,
    tot,
    sems,
):
    step = pl.program_id(0)
    limit = live_rows(counts_ref)

    @pl.when(step == 0)
    def _():
        w_all_t[0 : 2 * D, :] = w_in_ref[...].astype(F32).T.astype(BF16)
        w_all_t[2 * D :, :] = jnp.concatenate(
            [w_temp_ref[...], jnp.zeros((8, D), BF16)], axis=0
        )
        for group in range(2):
            sw_pad[...] = jnp.zeros_like(sw_pad)
            for j in range(4):
                sw_pad[32 * j : 32 * j + 32, 64 * j : 64 * j + 64] = sw_ref[
                    4 * group + j
                ].astype(F32)
            rows = sw_pad[...]
            sw_cols_ref[group] = rows.T.astype(BF16)
        acc[...] = jnp.zeros_like(acc)
        tot[...] = jnp.zeros_like(tot)

    here = pl.ds(pl.multiple_of(step * CHUNK, CHUNK), CHUNK)
    inside = inside_row(limit, step)
    points = points_ref[...]
    cot = cot_ref[...]
    projected = nt(w_all_t[...], points)
    gate = jax.nn.sigmoid(projected[2 * D : 2 * D + HEADS])
    gate_ref[:, here] = gate
    inv_temper = 1.0 / (0.5 + 1.5 * gate)
    proj_x = projected[0:D].astype(BF16)
    fx_ref[:, here] = proj_x
    proj_f = projected[D : 2 * D].astype(BF16)
    back = (nt(w_out_ref[...], cot) * inside).astype(BF16)
    for h in range(HEADS):
        fb_ref[64 * h : 64 * h + 32, here] = back[32 * h : 32 * h + 32]
        fb_ref[64 * h + 32 : 64 * h + 64, here] = proj_f[32 * h : 32 * h + 32]
    for group in range(2):
        raw = nn(sw_cols_ref[group], proj_x[128 * group : 128 * group + 128])
        raw_ref[256 * group : 256 * group + 256, here] = raw
        pieces = []
        for j in range(4):
            h = 4 * group + j
            logits = raw[64 * j : 64 * j + 64] * inv_temper[h : h + 1]
            top = jnp.max(logits, axis=0, keepdims=True)
            ex = jnp.exp(logits - top)
            shares = ex * (1.0 / jnp.sum(ex, axis=0, keepdims=True))
            shares_ref[64 * h : 64 * h + 64, here] = shares
            masked = shares * inside
            folded = masked[:, 0:128]
            for k in range(1, CHUNK // 128):
                folded = folded + masked[:, 128 * k : 128 * k + 128]
            tot[64 * h : 64 * h + 64, :] += folded
            pieces.append(masked.astype(BF16))
        rounded = jnp.concatenate(pieces, axis=0)
        acc[group] += nt(rounded, fb_ref[256 * group : 256 * group + 256, here])
        for copy in stash_copies(
            step, group, (fb_hbm, shares_hbm, raw_hbm), (fb_ref, shares_ref, raw_ref), sems, True
        ):
            copy.start()

    @pl.when(step == pl.num_programs(0) - 1)
    def _():
        low = lane_ids((32, 128)) < 64
        totals = nt(jnp.ones((8, 128), F32), tot[...], HIGH)
        for h in range(HEADS):
            group, j = divmod(h, 4)
            lanes = 128 * (j // 2)
            block = acc[group, 64 * j : 64 * j + 64, lanes : lanes + 128]
            upper, lower = block[0:32], block[32:64]
            row = totals[:, 128 * (h // 2) : 128 * (h // 2) + 128]
            if j % 2 == 0:
                both = jnp.where(low, upper, pltpu.roll(lower, 64, 1))
            else:
                both = jnp.where(low, pltpu.roll(upper, 64, 1), lower)
                row = pltpu.roll(row, 64, 1)
            packed_ref[h, 0:32, :] = both
            packed_ref[h, 32:40, :] = row
        for k in range(STEPS):
            for group in range(2):
                for copy in stash_copies(
                    k, group, (fb_hbm, shares_hbm, raw_hbm), (fb_ref, shares_ref, raw_ref), sems, True
                ):
                    copy.wait()


def forward_call(counts, points, cotangent, w_in, w_temp, slice_weight, w_out):
    whole = pl.BlockSpec(memory_space=pltpu.VMEM)
    far = pl.BlockSpec(memory_space=pltpu.HBM)
    row_block = pl.BlockSpec((CHUNK, D), lambda i: (i, 0))

    def fixed(shape):
        return pl.BlockSpec(shape, lambda i: (0,) * len(shape))

    return pl.pallas_call(
        forward_kernel,
        grid=(STEPS,),
        in_specs=[
            pl.BlockSpec(memory_space=pltpu.SMEM),
            row_block,
            row_block,
            fixed((D, 2 * D)),
            fixed((HEADS, D)),
            fixed((HEADS, WIDTH, SLICES)),
            fixed((D, D)),
        ],
        out_specs=[
            fixed((HEADS, 40, 128)),
            whole,
            whole,
            far,
            far,
            far,
        ],
        out_shape=[
            jax.ShapeDtypeStruct((HEADS, 40, 128), F32),
            jax.ShapeDtypeStruct((D, ROWS), BF16),
            jax.ShapeDtypeStruct((HEADS, ROWS), F32),
            pltpu.HBM((2 * D, ROWS), BF16),
            pltpu.HBM((2 * D, ROWS), F32),
            pltpu.HBM((2 * D, ROWS), F32),
        ],
        scratch_shapes=[
            pltpu.VMEM((2 * D, ROWS), BF16),
            pltpu.VMEM((2 * D, ROWS), F32),
            pltpu.VMEM((2 * D, ROWS), F32),
            pltpu.VMEM((2, 256, 128), BF16),
            pltpu.VMEM((2 * D + 16, D), BF16),
            pltpu.VMEM((128, 256), F32),
            pltpu.VMEM((2, 256, 256), F32),
            pltpu.VMEM((2 * D, 128), F32),
            pltpu.SemaphoreType.DMA((STEPS, 2, 3)),
        ],
        compiler_params=pltpu.CompilerParams(
            dimension_semantics=("arbitrary",), vmem_limit_bytes=VMEM_LIMIT
        ),
        name="forward",
    )(*in_hbm(counts, points, cotangent, w_in, w_temp.T, slice_weight, w_out))


def attention_kernel(parts_ref, qkv_ref, out_ref, grad_qkv_ref):
    summed = parts_ref[0]
    for k in range(1, parts_ref.shape[0]):
        summed = summed + parts_ref[k]
    pairs = jnp.concatenate([summed[0:32], pltpu.roll(summed[0:32], 64, 1)], axis=0)
    grad_att = pairs[:, 0:WIDTH]
    numer = pltpu.roll(pairs, 96, 1)[:, 0:WIDTH]
    totals = jnp.concatenate([summed[32:40]] * 16, axis=0).T[0:SLICES, 0:1]
    inv = 1.0 / (totals + EPSILON)
    tokens = numer * inv
    w_q, w_k, w_v = qkv_ref[0], qkv_ref[1], qkv_ref[2]
    scale = WIDTH**-0.5
    query = nn(tokens, w_q, HIGH)
    keys = nn(tokens, w_k, HIGH)
    values = nn(tokens, w_v, HIGH)
    scores = nt(query, keys, HIGH) * scale
    ex = jnp.exp(scores - jnp.max(scores, axis=1, keepdims=True))
    weights = ex / jnp.sum(ex, axis=1, keepdims=True)
    attended = nn(weights, values, HIGH)
    grad_values = tn(weights, grad_att, HIGH)
    grad_weights = nt(grad_att, values, HIGH)
    inner = jnp.sum(weights * grad_weights, axis=1, keepdims=True)
    grad_scores = weights * (grad_weights - inner) * scale
    grad_query = nn(grad_scores, keys, HIGH)
    grad_keys = tn(grad_scores, query, HIGH)
    grad_tokens = (
        nt(grad_query, w_q, HIGH) + nt(grad_keys, w_k, HIGH) + nt(grad_values, w_v, HIGH)
    )
    grad_qkv_ref[...] = jnp.zeros_like(grad_qkv_ref)
    for i, grad in enumerate((grad_query, grad_keys, grad_values)):
        grad_qkv_ref[:, WIDTH * i : WIDTH * i + WIDTH] = tn(tokens, grad, HIGH) * (1.0 / 32)
    grad_numer = grad_tokens * inv
    grad_totals = -jnp.sum(grad_tokens * tokens, axis=1, keepdims=True) * inv
    grad_row = jnp.broadcast_to(grad_totals, (SLICES, 128)).T[0:8]
    for k in range(out_ref.shape[0]):
        out_ref[k, 0:32, 0:32] = attended[0:32]
        out_ref[k, 0:32, 32:64] = grad_numer[0:32]
        out_ref[k, 0:32, 64:96] = attended[32:64]
        out_ref[k, 0:32, 96:128] = grad_numer[32:64]
        out_ref[k, 32:40, 0:64] = grad_row
        out_ref[k, 32:40, 64:128] = grad_row


def attention_call(parts, qkv_weight):
    whole = pl.BlockSpec(memory_space=pltpu.VMEM)
    return pl.pallas_call(
        attention_kernel,
        in_specs=[whole, whole],
        out_specs=[whole, whole],
        out_shape=[
            jax.ShapeDtypeStruct((SUBS, 40, 128), F32),
            jax.ShapeDtypeStruct((WIDTH, 128), F32),
        ],
        compiler_params=pltpu.CompilerParams(vmem_limit_bytes=SMALL_LIMIT),
        name="slice_attention",
    )(parts, qkv_weight)


def backward_kernel(
    counts_ref,
    points_ref,
    cot_ref,
    fx_ref,
    gate_ref,
    fb_hbm,
    shares_hbm,
    raw_hbm,
    sw_ref,
    heads_ref,
    grad_qkv_ref,
    w_in_ref,
    w_temp_ref,
    w_out_ref,
    b_out_ref,
    result_ref,
    grad_points_ref,
    mine_ref,
    theirs_ref,
    fb_ref,
    shares_ref,
    raw_ref,
    sw_rows_ref,
    token_pad,
    token_cols,
    token_rows,
    grad_tot,
    w_out_t,
    b_col,
    temp_pad,
    mixed_ref,
    proj_ref,
    acc_slice,
    acc_out,
    acc_in,
    sems,
):
    step = pl.program_id(0)
    limit = live_rows(counts_ref)

    @pl.when(step == 0)
    def _():
        for k in range(STEPS):
            for group in range(2):
                for copy in stash_copies(
                    k, group, (fb_hbm, shares_hbm, raw_hbm), (fb_ref, shares_ref, raw_ref), sems, False
                ):
                    copy.start()
        sw_rows_ref[...] = jnp.zeros_like(sw_rows_ref)
        for h in range(HEADS):
            group, j = divmod(h, 4)
            sw_rows_ref[group, 32 * j : 32 * j + 32, 64 * j : 64 * j + 64] = sw_ref[h]
        w_out_t[...] = w_out_ref[...].astype(F32).T.astype(BF16)
        b_col[...] = jnp.broadcast_to(b_out_ref[...], (128, D)).T[:, 0:1]
        temp_pad[...] = jnp.concatenate(
            [w_temp_ref[...].astype(F32), jnp.zeros((120, D), F32)], axis=0
        ).T.astype(BF16)
        rows = [heads_ref[h, 32:33, :] for h in range(HEADS)]
        square = jnp.concatenate(rows * 16, axis=0).T
        low = lane_ids((64, 128)) < 64
        for group in range(2):
            token_pad[...] = jnp.zeros_like(token_pad)
            for j in range(4):
                h = 4 * group + j
                both = heads_ref[h, 0:32, :]
                turned = pltpu.roll(both, 64, 1)
                lanes = 128 * (j // 2)
                if j % 2 == 0:
                    block = jnp.concatenate([both, turned], axis=0)
                    block = jnp.where(low, block, 0.0)
                else:
                    block = jnp.concatenate([turned, both], axis=0)
                    block = jnp.where(low, 0.0, block)
                token_pad[64 * j : 64 * j + 64, lanes : lanes + 128] = block
                grad_tot[64 * h : 64 * h + 64, :] = jnp.broadcast_to(
                    square[0:64, h : h + 1], (64, 128)
                )
            token_cols[group] = token_pad[...].astype(BF16)
            token_rows[group] = token_pad[...].T.astype(BF16)
        acc_slice[...] = jnp.zeros_like(acc_slice)
        acc_out[...] = jnp.zeros_like(acc_out)
        acc_in[...] = jnp.zeros_like(acc_in)

    here = pl.ds(pl.multiple_of(step * CHUNK, CHUNK), CHUNK)
    inside = inside_row(limit, step)
    points = points_ref[...]
    cot = cot_ref[...]
    gate = gate_ref[:, here]
    inv_temper = 1.0 / (0.5 + 1.5 * gate)
    scale_temp = -1.5 * gate * (1.0 - gate) * inv_temper
    temp_rows = []
    for group in range(2):
        for copy in stash_copies(
            step, group, (fb_hbm, shares_hbm, raw_hbm), (fb_ref, shares_ref, raw_ref), sems, False
        ):
            copy.wait()
        fx = fx_ref[128 * group : 128 * group + 128, here]
        raw = raw_ref[256 * group : 256 * group + 256, here]
        total = nn(token_cols[group], fb_ref[256 * group : 256 * group + 256, here])
        scaled_parts = []
        rounded_parts = []
        for j in range(4):
            h = 4 * group + j
            shares = shares_ref[64 * h : 64 * h + 64, here]
            gt = grad_tot[64 * h : 64 * h + 64, :]
            share_grad = total[64 * j : 64 * j + 64] + jnp.concatenate(
                [gt] * (CHUNK // 128), axis=1
            )
            weighted = shares * share_grad
            inner = jnp.sum(weighted, axis=0, keepdims=True)
            factor = inside * inv_temper[h : h + 1]
            scaled = shares * (share_grad - inner) * factor
            temp_rows.append(
                jnp.sum(scaled * raw[64 * j : 64 * j + 64], axis=0, keepdims=True)
                * scale_temp[h : h + 1]
            )
            scaled_parts.append(scaled.astype(BF16))
            rounded_parts.append((shares * inside).astype(BF16))
        scaled_bf = jnp.concatenate(scaled_parts, axis=0)
        rounded = jnp.concatenate(rounded_parts, axis=0)
        acc_slice[group] += nt(fx, scaled_bf)
        proj_ref[128 * group : 128 * group + 128, :] = nn(sw_rows_ref[group], scaled_bf).astype(
            BF16
        )
        pair = nn(token_rows[group], rounded).astype(BF16)
        for j in range(4):
            h = 4 * group + j
            mixed_ref[32 * h : 32 * h + 32, :] = pair[64 * j : 64 * j + 32]
            proj_ref[D + 32 * h : D + 32 * h + 32, :] = pair[64 * j + 32 : 64 * j + 64]
    temp_grad = jnp.concatenate(
        temp_rows + [jnp.zeros((8, CHUNK), F32)], axis=0
    ).astype(BF16)
    proj_ref[2 * D :, :] = temp_grad
    mixed = mixed_ref[0:D, :]
    out = nn(w_out_t[...], mixed) + b_col[...]
    result_ref[...] = (out * inside).astype(BF16).T
    mixed_ref[D:, :] = jnp.broadcast_to(inside, (16, CHUNK)).astype(BF16)
    acc_out[...] += nn(mixed_ref[...], cot)
    acc_in[...] += nn(proj_ref[...], points)
    grad = nn(w_in_ref[...], proj_ref[0 : 2 * D, :]) + nn(temp_pad[...][:, 0:16], temp_grad)
    grad_points_ref[...] = grad.astype(BF16).T

    @pl.when(step == pl.num_programs(0) - 1)
    def _():
        low = lane_ids((32, 128)) < 64

        def write_first(ref):
            for k in range(3):
                ref[256 * k : 256 * k + 256, :] = acc_in[128 * k : 128 * k + 128, :].T
            for k in range(4):
                group, pair = divmod(k, 2)
                block = acc_slice[group, 64 * pair : 64 * pair + 64, 128 * pair : 128 * pair + 128]
                ref[768 + 32 * k : 800 + 32 * k, :] = jnp.where(low, block[0:32], block[32:64])

        def write_second(ref):
            ref[0:256, :] = acc_in[384:512, :].T
            ref[256:512, :] = acc_out[0:256, 0:128]
            ref[512:768, :] = acc_out[0:256, 128:256]
            ref[768:776, :] = acc_in[512:520, 0:128]
            ref[776:784, :] = acc_in[512:520, 128:256]
            ref[784:792, :] = acc_out[256:264, 0:128]
            ref[792:800, :] = acc_out[256:264, 128:256]
            ref[800:832, :] = grad_qkv_ref[...]
            ref[832:HALF, :] = jnp.zeros((HALF - 832, 128), F32)

        core = device_place()[2]

        @pl.when(core == 0)
        def _():
            write_first(mine_ref)
            write_second(theirs_ref)

        @pl.when(core != 0)
        def _():
            write_first(theirs_ref)
            write_second(mine_ref)


def backward_call(counts, points, cotangent, stash, heads, grad_qkv, w_in, w_temp, slice_weight, w_out, b_out):
    fx, gate, fb, shares, raw = stash
    whole = pl.BlockSpec(memory_space=pltpu.VMEM)
    far = pl.BlockSpec(memory_space=pltpu.HBM)
    far = pl.BlockSpec(memory_space=pltpu.HBM)
    row_block = pl.BlockSpec((CHUNK, D), lambda i: (i, 0))

    def fixed(shape):
        return pl.BlockSpec(shape, lambda i: (0,) * len(shape))

    return pl.pallas_call(
        backward_kernel,
        grid=(STEPS,),
        in_specs=[
            pl.BlockSpec(memory_space=pltpu.SMEM),
            row_block,
            row_block,
            whole,
            whole,
            far,
            far,
            far,
            fixed((HEADS, WIDTH, SLICES)),
            fixed((HEADS, 40, 128)),
            fixed((WIDTH, 128)),
            fixed((D, 2 * D)),
            fixed((HEADS, D)),
            fixed((D, D)),
            fixed((1, D)),
        ],
        out_specs=[row_block, row_block, fixed((HALF, 128)), fixed((HALF, 128))],
        out_shape=[
            jax.ShapeDtypeStruct((ROWS, D), BF16),
            jax.ShapeDtypeStruct((ROWS, D), BF16),
            jax.ShapeDtypeStruct((HALF, 128), F32),
            jax.ShapeDtypeStruct((HALF, 128), F32),
        ],
        scratch_shapes=[
            pltpu.VMEM((2 * D, ROWS), BF16),
            pltpu.VMEM((2 * D, ROWS), F32),
            pltpu.VMEM((2 * D, ROWS), F32),
            pltpu.VMEM((2, 128, 256), BF16),
            pltpu.VMEM((256, 256), F32),
            pltpu.VMEM((2, 256, 256), BF16),
            pltpu.VMEM((2, 256, 256), BF16),
            pltpu.VMEM((2 * D, 128), F32),
            pltpu.VMEM((D, D), BF16),
            pltpu.VMEM((D, 1), F32),
            pltpu.VMEM((D, 128), BF16),
            pltpu.VMEM((D + 16, CHUNK), BF16),
            pltpu.VMEM((2 * D + 16, CHUNK), BF16),
            pltpu.VMEM((2, 128, 256), F32),
            pltpu.VMEM((D + 16, D), F32),
            pltpu.VMEM((2 * D + 16, D), F32),
            pltpu.SemaphoreType.DMA((STEPS, 2, 3)),
        ],
        compiler_params=pltpu.CompilerParams(
            dimension_semantics=("arbitrary",), vmem_limit_bytes=VMEM_LIMIT
        ),
        name="backward",
    )(
        *in_hbm(counts),
        points,
        cotangent,
        fx,
        gate,
        *in_hbm(fb, shares, raw, slice_weight),
        heads,
        *in_hbm(grad_qkv, w_in, w_temp.T, w_out, b_out.reshape(1, D)),
    )


def sum_spread(parts, copies):
    summed = jnp.sum(parts, axis=0)
    return jnp.broadcast_to(summed[None], (copies,) + summed.shape)


def unpack_kernel(
    mine_ref,
    theirs_ref,
    grad_in_ref,
    grad_temp_ref,
    grad_slice_ref,
    grad_out_ref,
    grad_bias_ref,
    grad_qkv_ref,
):
    def unpack(first, second):
        for k in range(3):
            grad_in_ref[:, 128 * k : 128 * k + 128] = first[256 * k : 256 * k + 256, :]
        grad_in_ref[:, 384:512] = second[0:256, :]
        for k in range(4):
            block = first[768 + 32 * k : 800 + 32 * k, :]
            grad_slice_ref[2 * k] = block[:, 0:64]
            grad_slice_ref[2 * k + 1] = pltpu.roll(block, 64, 1)[:, 0:64]
        grad_out_ref[:, 0:128] = second[256:512, :]
        grad_out_ref[:, 128:256] = second[512:768, :]
        for k in range(2):
            rows = second[768 + 8 * k : 776 + 8 * k, :]
            grad_temp_ref[:, 128 * k : 128 * k + 128] = rows
            grad_bias_ref[0:1, 128 * k : 128 * k + 128] = second[784 + 8 * k : 785 + 8 * k, :]
        qkv = second[800:832, :]
        grad_qkv_ref[0] = qkv[:, 0:32]
        grad_qkv_ref[1] = pltpu.roll(qkv, 96, 1)[:, 0:32]
        grad_qkv_ref[2] = pltpu.roll(qkv, 64, 1)[:, 0:32]

    core = device_place()[2]

    @pl.when(core == 0)
    def _():
        unpack(mine_ref, theirs_ref)

    @pl.when(core != 0)
    def _():
        unpack(theirs_ref, mine_ref)


def unpack_call(mine, theirs):
    whole = pl.BlockSpec(memory_space=pltpu.VMEM)
    return pl.pallas_call(
        unpack_kernel,
        in_specs=[whole, whole],
        out_specs=[whole] * 6,
        out_shape=[
            jax.ShapeDtypeStruct((D, 2 * D), F32),
            jax.ShapeDtypeStruct((HEADS, D), F32),
            jax.ShapeDtypeStruct((HEADS, WIDTH, SLICES), F32),
            jax.ShapeDtypeStruct((D, D), F32),
            jax.ShapeDtypeStruct((1, D), F32),
            jax.ShapeDtypeStruct((3, WIDTH, WIDTH), F32),
        ],
        compiler_params=pltpu.CompilerParams(vmem_limit_bytes=SMALL_LIMIT),
        name="unpack",
    )(mine, theirs)


def swap_cores(values):
    return lax.ppermute(values, "core", [(0, 1), (1, 0)])


def spread_over(values, axes):
    return lax.all_to_all(values, axes, 0, 0)


def per_device(points, cotangent, counts, w_in, w_temp, slice_weight, qkv_weight, w_out, b_out):
    packed, *stash = forward_call(
        counts, points, cotangent, w_in, w_temp, slice_weight, w_out
    )
    packed = packed + swap_cores(packed)
    parts = sum_spread(spread_over(packed, "sub"), 16)
    parts = spread_over(parts, ("x", "y"))
    heads, grad_qkv = attention_call(parts, qkv_weight)
    heads = spread_over(heads, "sub")
    result, grad_points, mine, theirs = backward_call(
        counts, points, cotangent, stash, heads, grad_qkv, w_in, w_temp, slice_weight, w_out, b_out
    )
    mine = (mine + swap_cores(theirs)).reshape(16, HALF // 16, 128)
    mine = sum_spread(spread_over(mine, ("x", "y")), SUBS)
    mine = sum_spread(spread_over(mine, "sub"), 16)
    mine = spread_over(mine, ("x", "y")).reshape(HALF, 128)
    grad_w_in, grad_w_temp, grad_slice, grad_w_out, grad_bias, grad_qkv = unpack_call(mine, swap_cores(mine))
    return (
        result,
        grad_points,
        grad_w_in,
        grad_w_temp.T,
        grad_slice,
        grad_w_out,
        grad_bias.reshape(D),
        grad_qkv,
    )


def solution(mesh):
    fine = Mesh(mesh.devices.reshape(4, 4, 2, 8), ("x", "y", "core", "sub"))
    rows = P(("x", "y", "core", "sub"), None)
    return jax.shard_map(
        per_device,
        mesh=fine,
        in_specs=(rows, rows) + (P(),) * 7,
        out_specs=(rows, rows) + (P(),) * 6,
        check_vma=False,
    )
```

```python
import jax
import jax.numpy as jnp
from jax import lax
from jax.experimental import pallas as pl
from jax.experimental.pallas import tpu as pltpu
from jax.sharding import Mesh, PartitionSpec as P

EPSILON = 1e-05
F32 = jnp.float32
BF16 = jnp.bfloat16
HIGH = lax.Precision.HIGHEST

D = 256
HEADS = 8
SLICES = 64
WIDTH = 32
ROWS = 2048
SUBS = 8
HALF = 896
VMEM_LIMIT = 40 * 1024 * 1024
SMALL_LIMIT = 16 * 1024 * 1024


def nn(a, b, precision=None):
    return lax.dot_general(
        a, b, (((1,), (0,)), ((), ())), preferred_element_type=F32, precision=precision
    )


def nt(a, b, precision=None):
    return lax.dot_general(
        a, b, (((1,), (1,)), ((), ())), preferred_element_type=F32, precision=precision
    )


def tn(a, b, precision=None):
    return lax.dot_general(
        a, b, (((0,), (0,)), ((), ())), preferred_element_type=F32, precision=precision
    )


def lane_ids(shape):
    return lax.broadcasted_iota(jnp.int32, shape, 1)


def device_place():
    x, y = lax.axis_index("x"), lax.axis_index("y")
    core, sub = lax.axis_index("core"), lax.axis_index("sub")
    return (x * 4 + y) * 2 + core, sub, core


def live_rows(counts_ref):
    dom, sub, _ = device_place()
    return counts_ref[dom] - sub * ROWS


def in_hbm(*arrays):
    return [pltpu.with_memory_space_constraint(a, pltpu.HBM) for a in arrays]


def inside_row(counts_ref):
    return jnp.where(lane_ids((1, ROWS)) < live_rows(counts_ref), 1.0, 0.0).astype(F32)


def forward_kernel(
    counts_ref,
    points_ref,
    cot_ref,
    w_in_ref,
    w_temp_ref,
    sw_ref,
    w_out_ref,
    packed_ref,
    fx_ref,
    gate_ref,
    top_ref,
    scale_ref,
    fb_ref,
    sw_cols_ref,
    w_all_t,
    sw_pad,
):
    w_all_t[0 : 2 * D, :] = w_in_ref[...].astype(F32).T.astype(BF16)
    w_all_t[2 * D :, :] = jnp.concatenate([w_temp_ref[...], jnp.zeros((8, D), BF16)], axis=0)
    for group in range(2):
        sw_pad[...] = jnp.zeros_like(sw_pad)
        for j in range(4):
            sw_pad[32 * j : 32 * j + 32, 64 * j : 64 * j + 64] = sw_ref[4 * group + j].astype(F32)
        sw_cols_ref[group] = sw_pad[...].T.astype(BF16)
    inside = inside_row(counts_ref)
    projected = nt(w_all_t[...], points_ref[...])
    gate = jax.nn.sigmoid(projected[2 * D : 2 * D + HEADS])
    gate_ref[...] = gate
    inv_temper = 1.0 / (0.5 + 1.5 * gate)
    proj_x = projected[0:D].astype(BF16)
    fx_ref[...] = proj_x
    for h in range(HEADS):
        fb_ref[64 * h + 32 : 64 * h + 64, :] = projected[D + 32 * h : D + 32 * h + 32].astype(BF16)
    back = (nt(w_out_ref[...], cot_ref[...]) * inside).astype(BF16)
    for h in range(HEADS):
        fb_ref[64 * h : 64 * h + 32, :] = back[32 * h : 32 * h + 32]
    sums = []
    folds = []
    for group in range(2):
        raw = nn(sw_cols_ref[group], proj_x[128 * group : 128 * group + 128])
        pieces = []
        for j in range(4):
            h = 4 * group + j
            logits = raw[64 * j : 64 * j + 64] * inv_temper[h : h + 1]
            top = jnp.max(logits, axis=0, keepdims=True)
            ex = jnp.exp(logits - top)
            scale = 1.0 / jnp.sum(ex, axis=0, keepdims=True)
            top_ref[h : h + 1, :] = top
            scale_ref[h : h + 1, :] = scale
            shares = ex * scale
            masked = shares * inside
            folded = masked[:, 0:128]
            for k in range(1, ROWS // 128):
                folded = folded + masked[:, 128 * k : 128 * k + 128]
            folds.append(folded)
            pieces.append(masked.astype(BF16))
        rounded = jnp.concatenate(pieces, axis=0)
        sums.append(nt(rounded, fb_ref[256 * group : 256 * group + 256, :]))
    low = lane_ids((32, 128)) < 64
    totals = nt(jnp.ones((8, 128), F32), jnp.concatenate(folds, axis=0), HIGH)
    for h in range(HEADS):
        group, j = divmod(h, 4)
        lanes = 128 * (j // 2)
        block = sums[group][64 * j : 64 * j + 64, lanes : lanes + 128]
        upper, lower = block[0:32], block[32:64]
        row = totals[:, 128 * (h // 2) : 128 * (h // 2) + 128]
        if j % 2 == 0:
            both = jnp.where(low, upper, pltpu.roll(lower, 64, 1))
        else:
            both = jnp.where(low, pltpu.roll(upper, 64, 1), lower)
            row = pltpu.roll(row, 64, 1)
        packed_ref[h, 0:32, :] = both
        packed_ref[h, 32:40, :] = row


def forward_call(counts, points, cotangent, w_in, w_temp, slice_weight, w_out):
    whole = pl.BlockSpec(memory_space=pltpu.VMEM)
    far = pl.BlockSpec(memory_space=pltpu.HBM)
    block = pl.BlockSpec()
    return pl.pallas_call(
        forward_kernel,
        in_specs=[pl.BlockSpec(memory_space=pltpu.SMEM)] + [block] * 6,
        out_specs=[whole] * 6,
        out_shape=[
            jax.ShapeDtypeStruct((HEADS, 40, 128), F32),
            jax.ShapeDtypeStruct((D, ROWS), BF16),
            jax.ShapeDtypeStruct((HEADS, ROWS), F32),
            jax.ShapeDtypeStruct((HEADS, ROWS), F32),
            jax.ShapeDtypeStruct((HEADS, ROWS), F32),
            jax.ShapeDtypeStruct((2 * D, ROWS), BF16),
        ],
        scratch_shapes=[
            pltpu.VMEM((2, 256, 128), BF16),
            pltpu.VMEM((2 * D + 16, D), BF16),
            pltpu.VMEM((128, 256), F32),
        ],
        compiler_params=pltpu.CompilerParams(vmem_limit_bytes=VMEM_LIMIT),
        name="forward",
    )(*in_hbm(counts, points, cotangent, w_in, w_temp.T, slice_weight, w_out))


def attention_kernel(parts_ref, qkv_ref, out_ref, grad_qkv_ref):
    summed = parts_ref[0]
    for k in range(1, parts_ref.shape[0]):
        summed = summed + parts_ref[k]
    pairs = jnp.concatenate([summed[0:32], pltpu.roll(summed[0:32], 64, 1)], axis=0)
    grad_att = pairs[:, 0:WIDTH]
    numer = pltpu.roll(pairs, 96, 1)[:, 0:WIDTH]
    totals = jnp.concatenate([summed[32:40]] * 16, axis=0).T[0:SLICES, 0:1]
    inv = 1.0 / (totals + EPSILON)
    tokens = numer * inv
    w_q, w_k, w_v = qkv_ref[0], qkv_ref[1], qkv_ref[2]
    scale = WIDTH**-0.5
    query = nn(tokens, w_q, HIGH)
    keys = nn(tokens, w_k, HIGH)
    values = nn(tokens, w_v, HIGH)
    scores = nt(query, keys, HIGH) * scale
    ex = jnp.exp(scores - jnp.max(scores, axis=1, keepdims=True))
    weights = ex / jnp.sum(ex, axis=1, keepdims=True)
    attended = nn(weights, values, HIGH)
    grad_values = tn(weights, grad_att, HIGH)
    grad_weights = nt(grad_att, values, HIGH)
    inner = jnp.sum(weights * grad_weights, axis=1, keepdims=True)
    grad_scores = weights * (grad_weights - inner) * scale
    grad_query = nn(grad_scores, keys, HIGH)
    grad_keys = tn(grad_scores, query, HIGH)
    grad_tokens = (
        nt(grad_query, w_q, HIGH) + nt(grad_keys, w_k, HIGH) + nt(grad_values, w_v, HIGH)
    )
    grad_qkv_ref[...] = jnp.zeros_like(grad_qkv_ref)
    for i, grad in enumerate((grad_query, grad_keys, grad_values)):
        grad_qkv_ref[:, WIDTH * i : WIDTH * i + WIDTH] = tn(tokens, grad, HIGH) * (1.0 / 32)
    grad_numer = grad_tokens * inv
    grad_totals = -jnp.sum(grad_tokens * tokens, axis=1, keepdims=True) * inv
    grad_row = jnp.broadcast_to(grad_totals, (SLICES, 128)).T[0:8]
    for k in range(out_ref.shape[0]):
        out_ref[k, 0:32, 0:32] = attended[0:32]
        out_ref[k, 0:32, 32:64] = grad_numer[0:32]
        out_ref[k, 0:32, 64:96] = attended[32:64]
        out_ref[k, 0:32, 96:128] = grad_numer[32:64]
        out_ref[k, 32:40, 0:64] = grad_row
        out_ref[k, 32:40, 64:128] = grad_row


def attention_call(parts, qkv_weight):
    whole = pl.BlockSpec(memory_space=pltpu.VMEM)
    return pl.pallas_call(
        attention_kernel,
        in_specs=[whole, whole],
        out_specs=[whole, whole],
        out_shape=[
            jax.ShapeDtypeStruct((SUBS, 40, 128), F32),
            jax.ShapeDtypeStruct((WIDTH, 128), F32),
        ],
        compiler_params=pltpu.CompilerParams(vmem_limit_bytes=SMALL_LIMIT),
        name="slice_attention",
    )(parts, qkv_weight)


def backward_kernel(
    counts_ref,
    points_hbm,
    cot_hbm,
    fx_ref,
    gate_ref,
    top_ref,
    scale_ref,
    fb_ref,
    sw_ref,
    w_in_ref,
    w_temp_ref,
    w_out_ref,
    b_out_ref,
    heads_ref,
    grad_qkv_ref,
    result_hbm,
    grad_points_hbm,
    mine_ref,
    theirs_ref,
    result_ref,
    grad_points_ref,
    mixed_ref,
    proj_ref,
    points_ref,
    cot_ref,
    sw_rows_ref,
    token_pad,
    token_cols,
    token_rows,
    grad_tot,
    sems,
):
    get_points = pltpu.make_async_copy(points_hbm, points_ref, sems.at[0])
    get_cot = pltpu.make_async_copy(cot_hbm, cot_ref, sems.at[1])
    put_result = pltpu.make_async_copy(result_ref, result_hbm, sems.at[2])
    put_grad = pltpu.make_async_copy(grad_points_ref, grad_points_hbm, sems.at[3])
    get_points.start()
    get_cot.start()
    sw_rows_ref[...] = jnp.zeros_like(sw_rows_ref)
    for h in range(HEADS):
        group, j = divmod(h, 4)
        sw_rows_ref[group, 32 * j : 32 * j + 32, 64 * j : 64 * j + 64] = sw_ref[h]
    rows = [heads_ref[h, 32:33, :] for h in range(HEADS)]
    square = jnp.concatenate(rows * 16, axis=0).T
    low = lane_ids((64, 128)) < 64
    for group in range(2):
        token_pad[...] = jnp.zeros_like(token_pad)
        for j in range(4):
            h = 4 * group + j
            both = heads_ref[h, 0:32, :]
            turned = pltpu.roll(both, 64, 1)
            lanes = 128 * (j // 2)
            if j % 2 == 0:
                block = jnp.where(low, jnp.concatenate([both, turned], axis=0), 0.0)
            else:
                block = jnp.where(low, 0.0, jnp.concatenate([turned, both], axis=0))
            token_pad[64 * j : 64 * j + 64, lanes : lanes + 128] = block
            grad_tot[64 * h : 64 * h + 64, :] = jnp.broadcast_to(square[0:64, h : h + 1], (64, 128))
        token_cols[group] = token_pad[...].astype(BF16)
        token_rows[group] = token_pad[...].T.astype(BF16)

    inside = inside_row(counts_ref)
    gate = gate_ref[...]
    inv_temper = 1.0 / (0.5 + 1.5 * gate)
    scale_temp = -1.5 * gate * (1.0 - gate) * inv_temper
    b_col = jnp.broadcast_to(b_out_ref[...], (128, D)).T[:, 0:1]
    w_out_t = w_out_ref[...].astype(F32).T.astype(BF16)
    temp_cols = jnp.concatenate([w_temp_ref[...].astype(F32), jnp.zeros((120, D), F32)], axis=0).T
    temp_cols = temp_cols[:, 0:16].astype(BF16)
    temp_rows = []
    slices = []
    for group in range(2):
        fx = fx_ref[128 * group : 128 * group + 128, :]
        raw = tn(sw_rows_ref[group], fx)
        total = nn(token_cols[group], fb_ref[256 * group : 256 * group + 256, :])
        scaled_parts = []
        rounded_parts = []
        for j in range(4):
            h = 4 * group + j
            rows = slice(64 * j, 64 * j + 64)
            logits = raw[rows] * inv_temper[h : h + 1]
            shares = jnp.exp(logits - top_ref[h : h + 1, :]) * scale_ref[h : h + 1, :]
            gt = grad_tot[64 * h : 64 * h + 64, :]
            share_grad = total[rows] + jnp.concatenate([gt] * (ROWS // 128), axis=1)
            inner = jnp.sum(shares * share_grad, axis=0, keepdims=True)
            scaled = shares * (share_grad - inner) * (inside * inv_temper[h : h + 1])
            temp_rows.append(
                jnp.sum(scaled * raw[rows], axis=0, keepdims=True) * scale_temp[h : h + 1]
            )
            scaled_parts.append(scaled.astype(BF16))
            rounded_parts.append((shares * inside).astype(BF16))
        scaled_bf = jnp.concatenate(scaled_parts, axis=0)
        slices.append(nt(fx, scaled_bf))
        proj_ref[128 * group : 128 * group + 128, :] = nn(sw_rows_ref[group], scaled_bf).astype(
            BF16
        )
        pair = nn(token_rows[group], jnp.concatenate(rounded_parts, axis=0)).astype(BF16)
        for j in range(4):
            h = 4 * group + j
            mixed_ref[32 * h : 32 * h + 32, :] = pair[64 * j : 64 * j + 32]
            proj_ref[D + 32 * h : D + 32 * h + 32, :] = pair[64 * j + 32 : 64 * j + 64]
    mixed_ref[D:, :] = jnp.broadcast_to(inside, (16, ROWS)).astype(BF16)
    out = nn(w_out_t, mixed_ref[0:D, :]) + b_col
    result_ref[...] = (out * inside).astype(BF16).T
    proj_ref[2 * D :, :] = jnp.concatenate(
        temp_rows + [jnp.zeros((8, ROWS), F32)], axis=0
    ).astype(BF16)
    grad = nn(w_in_ref[...], proj_ref[0 : 2 * D, :]) + nn(temp_cols, proj_ref[2 * D :, :])
    grad_points_ref[...] = grad.astype(BF16).T
    put_result.start()
    put_grad.start()
    get_points.wait()
    get_cot.wait()
    sum_out = nn(mixed_ref[...], cot_ref[...])
    sum_in = nn(proj_ref[...], points_ref[...])
    turned_in = [sum_in[128 * k : 128 * k + 128, :].T for k in range(4)]
    low = lane_ids((32, 128)) < 64

    def write_first(ref):
        for k in range(3):
            ref[256 * k : 256 * k + 256, :] = turned_in[k]
        for k in range(4):
            group, pair = divmod(k, 2)
            block = slices[group][64 * pair : 64 * pair + 64, 128 * pair : 128 * pair + 128]
            ref[768 + 32 * k : 800 + 32 * k, :] = jnp.where(low, block[0:32], block[32:64])

    def write_second(ref):
        ref[0:256, :] = turned_in[3]
        ref[256:512, :] = sum_out[0:256, 0:128]
        ref[512:768, :] = sum_out[0:256, 128:256]
        ref[768:776, :] = sum_in[512:520, 0:128]
        ref[776:784, :] = sum_in[512:520, 128:256]
        ref[784:792, :] = sum_out[256:264, 0:128]
        ref[792:800, :] = sum_out[256:264, 128:256]
        ref[800:832, :] = grad_qkv_ref[...]
        ref[832:HALF, :] = jnp.zeros((HALF - 832, 128), F32)

    core = device_place()[2]

    @pl.when(core == 0)
    def _():
        write_first(mine_ref)
        write_second(theirs_ref)

    @pl.when(core != 0)
    def _():
        write_first(theirs_ref)
        write_second(mine_ref)

    put_result.wait()
    put_grad.wait()


def backward_call(
    counts, points, cotangent, stash, heads, grad_qkv, w_in, w_temp, slice_weight, w_out, b_out
):
    whole = pl.BlockSpec(memory_space=pltpu.VMEM)
    far = pl.BlockSpec(memory_space=pltpu.HBM)
    block = pl.BlockSpec()
    return pl.pallas_call(
        backward_kernel,
        in_specs=[pl.BlockSpec(memory_space=pltpu.SMEM), far, far] + [whole] * 5
        + [block] * 5
        + [whole, whole],
        out_specs=[far, far, whole, whole],
        out_shape=[
            pltpu.HBM((ROWS, D), BF16),
            pltpu.HBM((ROWS, D), BF16),
            jax.ShapeDtypeStruct((HALF, 128), F32),
            jax.ShapeDtypeStruct((HALF, 128), F32),
        ],
        scratch_shapes=[
            pltpu.VMEM((ROWS, D), BF16),
            pltpu.VMEM((ROWS, D), BF16),
            pltpu.VMEM((D + 16, ROWS), BF16),
            pltpu.VMEM((2 * D + 16, ROWS), BF16),
            pltpu.VMEM((ROWS, D), BF16),
            pltpu.VMEM((ROWS, D), BF16),
            pltpu.VMEM((2, 128, 256), BF16),
            pltpu.VMEM((256, 256), F32),
            pltpu.VMEM((2, 256, 256), BF16),
            pltpu.VMEM((2, 256, 256), BF16),
            pltpu.VMEM((2 * D, 128), F32),
            pltpu.SemaphoreType.DMA((4,)),
        ],
        compiler_params=pltpu.CompilerParams(vmem_limit_bytes=VMEM_LIMIT),
        name="backward",
    )(
        *in_hbm(counts, points, cotangent),
        *stash,
        *in_hbm(slice_weight, w_in, w_temp.T, w_out, b_out.reshape(1, D)),
        heads,
        grad_qkv,
    )


def sum_spread(parts, copies):
    summed = jnp.sum(parts, axis=0)
    return jnp.broadcast_to(summed[None], (copies,) + summed.shape)


def unpack_kernel(
    mine_ref,
    theirs_ref,
    grad_in_ref,
    grad_temp_ref,
    grad_slice_ref,
    grad_out_ref,
    grad_bias_ref,
    grad_qkv_ref,
):
    def unpack(first, second):
        for k in range(3):
            grad_in_ref[:, 128 * k : 128 * k + 128] = first[256 * k : 256 * k + 256, :]
        grad_in_ref[:, 384:512] = second[0:256, :]
        for k in range(4):
            block = first[768 + 32 * k : 800 + 32 * k, :]
            grad_slice_ref[2 * k] = block[:, 0:64]
            grad_slice_ref[2 * k + 1] = pltpu.roll(block, 64, 1)[:, 0:64]
        grad_out_ref[:, 0:128] = second[256:512, :]
        grad_out_ref[:, 128:256] = second[512:768, :]
        for k in range(2):
            rows = second[768 + 8 * k : 776 + 8 * k, :]
            grad_temp_ref[:, 128 * k : 128 * k + 128] = rows
            grad_bias_ref[0:1, 128 * k : 128 * k + 128] = second[784 + 8 * k : 785 + 8 * k, :]
        qkv = second[800:832, :]
        grad_qkv_ref[0] = qkv[:, 0:32]
        grad_qkv_ref[1] = pltpu.roll(qkv, 96, 1)[:, 0:32]
        grad_qkv_ref[2] = pltpu.roll(qkv, 64, 1)[:, 0:32]

    core = device_place()[2]

    @pl.when(core == 0)
    def _():
        unpack(mine_ref, theirs_ref)

    @pl.when(core != 0)
    def _():
        unpack(theirs_ref, mine_ref)


def unpack_call(mine, theirs):
    whole = pl.BlockSpec(memory_space=pltpu.VMEM)
    return pl.pallas_call(
        unpack_kernel,
        in_specs=[whole, whole],
        out_specs=[whole] * 6,
        out_shape=[
            jax.ShapeDtypeStruct((D, 2 * D), F32),
            jax.ShapeDtypeStruct((HEADS, D), F32),
            jax.ShapeDtypeStruct((HEADS, WIDTH, SLICES), F32),
            jax.ShapeDtypeStruct((D, D), F32),
            jax.ShapeDtypeStruct((1, D), F32),
            jax.ShapeDtypeStruct((3, WIDTH, WIDTH), F32),
        ],
        compiler_params=pltpu.CompilerParams(vmem_limit_bytes=SMALL_LIMIT),
        name="unpack",
    )(mine, theirs)


def swap_cores(values):
    return lax.ppermute(values, "core", [(0, 1), (1, 0)])


def spread_over(values, axes):
    return lax.all_to_all(values, axes, 0, 0)


def per_device(points, cotangent, counts, w_in, w_temp, slice_weight, qkv_weight, w_out, b_out):
    packed, *stash = forward_call(counts, points, cotangent, w_in, w_temp, slice_weight, w_out)
    packed = packed + swap_cores(packed)
    parts = sum_spread(spread_over(packed, "sub"), 16)
    parts = spread_over(parts, ("x", "y"))
    heads, grad_qkv = attention_call(parts, qkv_weight)
    heads = spread_over(heads, "sub")
    result, grad_points, mine, theirs = backward_call(
        counts,
        points,
        cotangent,
        stash,
        heads,
        grad_qkv,
        w_in,
        w_temp,
        slice_weight,
        w_out,
        b_out,
    )
    mine = (mine + swap_cores(theirs)).reshape(16, HALF // 16, 128)
    mine = sum_spread(spread_over(mine, ("x", "y")), SUBS)
    mine = sum_spread(spread_over(mine, "sub"), 16)
    mine = spread_over(mine, ("x", "y")).reshape(HALF, 128)
    theirs = swap_cores(mine)
    grad_w_in, grad_w_temp, grad_slice, grad_w_out, grad_bias, grad_qkv = unpack_call(mine, theirs)
    return (
        result,
        grad_points,
        grad_w_in,
        grad_w_temp.T,
        grad_slice,
        grad_w_out,
        grad_bias.reshape(D),
        grad_qkv,
    )


def solution(mesh):
    fine = Mesh(mesh.devices.reshape(4, 4, 2, 8), ("x", "y", "core", "sub"))
    rows = P(("x", "y", "core", "sub"), None)
    return jax.shard_map(
        per_device,
        mesh=fine,
        in_specs=(rows, rows) + (P(),) * 7,
        out_specs=(rows, rows) + (P(),) * 6,
        check_vma=False,
    )
```

```python
import jax
import jax.numpy as jnp
from jax import lax
from jax.experimental import pallas as pl
from jax.experimental.pallas import tpu as pltpu
from jax.sharding import Mesh, PartitionSpec as P

EPSILON = 1e-05
F32 = jnp.float32
BF16 = jnp.bfloat16
HIGH = lax.Precision.HIGHEST

D = 256
HEADS = 8
SLICES = 64
WIDTH = 32
ROWS = 2048
SUBS = 8
HALF = 896
VMEM_LIMIT = 40 * 1024 * 1024
SMALL_LIMIT = 16 * 1024 * 1024


def nn(a, b, precision=None):
    return lax.dot_general(
        a, b, (((1,), (0,)), ((), ())), preferred_element_type=F32, precision=precision
    )


def nt(a, b, precision=None):
    return lax.dot_general(
        a, b, (((1,), (1,)), ((), ())), preferred_element_type=F32, precision=precision
    )


def tn(a, b, precision=None):
    return lax.dot_general(
        a, b, (((0,), (0,)), ((), ())), preferred_element_type=F32, precision=precision
    )


def lane_ids(shape):
    return lax.broadcasted_iota(jnp.int32, shape, 1)


def device_place():
    x, y = lax.axis_index("x"), lax.axis_index("y")
    core, sub = lax.axis_index("core"), lax.axis_index("sub")
    return (x * 4 + y) * 2 + core, sub, core


def live_rows(counts_ref):
    dom, sub, _ = device_place()
    return counts_ref[dom] - sub * ROWS


def in_hbm(*arrays):
    return [pltpu.with_memory_space_constraint(a, pltpu.HBM) for a in arrays]


def inside_row(counts_ref):
    return jnp.where(lane_ids((1, ROWS)) < live_rows(counts_ref), 1.0, 0.0).astype(F32)


def forward_kernel(
    counts_ref,
    points_ref,
    cot_ref,
    w_in_ref,
    w_temp_ref,
    sw_ref,
    w_out_ref,
    packed_ref,
    fx_ref,
    gate_ref,
    top_ref,
    scale_ref,
    fb_ref,
    sw_cols_ref,
    w_all_t,
    sw_pad,
):
    w_all_t[0 : 2 * D, :] = w_in_ref[...].astype(F32).T.astype(BF16)
    w_all_t[2 * D :, :] = jnp.concatenate([w_temp_ref[...], jnp.zeros((8, D), BF16)], axis=0)
    for group in range(2):
        sw_pad[...] = jnp.zeros_like(sw_pad)
        for j in range(4):
            sw_pad[32 * j : 32 * j + 32, 64 * j : 64 * j + 64] = sw_ref[4 * group + j].astype(F32)
        sw_cols_ref[group] = sw_pad[...].T.astype(BF16)
    inside = inside_row(counts_ref)
    projected = nt(w_all_t[...], points_ref[...])
    gate = jax.nn.sigmoid(projected[2 * D : 2 * D + HEADS])
    gate_ref[...] = gate
    inv_temper = 1.0 / (0.5 + 1.5 * gate)
    proj_x = projected[0:D].astype(BF16)
    fx_ref[...] = proj_x
    for h in range(HEADS):
        fb_ref[64 * h + 32 : 64 * h + 64, :] = projected[D + 32 * h : D + 32 * h + 32].astype(BF16)
    back = (nt(w_out_ref[...], cot_ref[...]) * inside).astype(BF16)
    for h in range(HEADS):
        fb_ref[64 * h : 64 * h + 32, :] = back[32 * h : 32 * h + 32]
    sums = []
    folds = []
    for group in range(2):
        raw = nn(sw_cols_ref[group], proj_x[128 * group : 128 * group + 128])
        pieces = []
        for j in range(4):
            h = 4 * group + j
            logits = raw[64 * j : 64 * j + 64] * inv_temper[h : h + 1]
            top = jnp.max(logits, axis=0, keepdims=True)
            ex = jnp.exp(logits - top)
            scale = 1.0 / jnp.sum(ex, axis=0, keepdims=True)
            top_ref[h : h + 1, :] = top
            scale_ref[h : h + 1, :] = scale
            shares = ex * scale
            masked = shares * inside
            folded = masked[:, 0:128]
            for k in range(1, ROWS // 128):
                folded = folded + masked[:, 128 * k : 128 * k + 128]
            folds.append(folded)
            pieces.append(masked.astype(BF16))
        rounded = jnp.concatenate(pieces, axis=0)
        sums.append(nt(rounded, fb_ref[256 * group : 256 * group + 256, :]))
    low = lane_ids((32, 128)) < 64
    totals = nt(jnp.ones((8, 128), F32), jnp.concatenate(folds, axis=0), HIGH)
    for h in range(HEADS):
        group, j = divmod(h, 4)
        lanes = 128 * (j // 2)
        block = sums[group][64 * j : 64 * j + 64, lanes : lanes + 128]
        upper, lower = block[0:32], block[32:64]
        row = totals[:, 128 * (h // 2) : 128 * (h // 2) + 128]
        if j % 2 == 0:
            both = jnp.where(low, upper, pltpu.roll(lower, 64, 1))
        else:
            both = jnp.where(low, pltpu.roll(upper, 64, 1), lower)
            row = pltpu.roll(row, 64, 1)
        packed_ref[h, 0:32, :] = both
        packed_ref[h, 32:40, :] = row


def forward_call(counts, points, cotangent, w_in, w_temp, slice_weight, w_out):
    whole = pl.BlockSpec(memory_space=pltpu.VMEM)
    far = pl.BlockSpec(memory_space=pltpu.HBM)
    block = pl.BlockSpec()
    return pl.pallas_call(
        forward_kernel,
        in_specs=[pl.BlockSpec(memory_space=pltpu.SMEM)] + [block] * 6,
        out_specs=[whole] * 6,
        out_shape=[
            jax.ShapeDtypeStruct((HEADS, 40, 128), F32),
            jax.ShapeDtypeStruct((D, ROWS), BF16),
            jax.ShapeDtypeStruct((HEADS, ROWS), F32),
            jax.ShapeDtypeStruct((HEADS, ROWS), F32),
            jax.ShapeDtypeStruct((HEADS, ROWS), F32),
            jax.ShapeDtypeStruct((2 * D, ROWS), BF16),
        ],
        scratch_shapes=[
            pltpu.VMEM((2, 256, 128), BF16),
            pltpu.VMEM((2 * D + 16, D), BF16),
            pltpu.VMEM((128, 256), F32),
        ],
        compiler_params=pltpu.CompilerParams(vmem_limit_bytes=VMEM_LIMIT),
        name="forward",
    )(*in_hbm(counts, points, cotangent, w_in, w_temp.T, slice_weight, w_out))


def attention_kernel(parts_ref, qkv_ref, out_ref, grad_qkv_ref):
    summed = parts_ref[0]
    for k in range(1, parts_ref.shape[0]):
        summed = summed + parts_ref[k]
    pairs = jnp.concatenate([summed[0:32], pltpu.roll(summed[0:32], 64, 1)], axis=0)
    grad_att = pairs[:, 0:WIDTH]
    numer = pltpu.roll(pairs, 96, 1)[:, 0:WIDTH]
    totals = jnp.concatenate([summed[32:40]] * 16, axis=0).T[0:SLICES, 0:1]
    inv = 1.0 / (totals + EPSILON)
    tokens = numer * inv
    w_q, w_k, w_v = qkv_ref[0], qkv_ref[1], qkv_ref[2]
    scale = WIDTH**-0.5
    query = nn(tokens, w_q, HIGH)
    keys = nn(tokens, w_k, HIGH)
    values = nn(tokens, w_v, HIGH)
    scores = nt(query, keys, HIGH) * scale
    ex = jnp.exp(scores - jnp.max(scores, axis=1, keepdims=True))
    weights = ex / jnp.sum(ex, axis=1, keepdims=True)
    attended = nn(weights, values, HIGH)
    grad_values = tn(weights, grad_att, HIGH)
    grad_weights = nt(grad_att, values, HIGH)
    inner = jnp.sum(weights * grad_weights, axis=1, keepdims=True)
    grad_scores = weights * (grad_weights - inner) * scale
    grad_query = nn(grad_scores, keys, HIGH)
    grad_keys = tn(grad_scores, query, HIGH)
    grad_tokens = (
        nt(grad_query, w_q, HIGH) + nt(grad_keys, w_k, HIGH) + nt(grad_values, w_v, HIGH)
    )
    grad_qkv_ref[...] = jnp.zeros_like(grad_qkv_ref)
    for i, grad in enumerate((grad_query, grad_keys, grad_values)):
        grad_qkv_ref[:, WIDTH * i : WIDTH * i + WIDTH] = tn(tokens, grad, HIGH) * (1.0 / 32)
    grad_numer = grad_tokens * inv
    grad_totals = -jnp.sum(grad_tokens * tokens, axis=1, keepdims=True) * inv
    grad_row = jnp.broadcast_to(grad_totals, (SLICES, 128)).T[0:8]
    for k in range(out_ref.shape[0]):
        out_ref[k, 0:32, 0:32] = attended[0:32]
        out_ref[k, 0:32, 32:64] = grad_numer[0:32]
        out_ref[k, 0:32, 64:96] = attended[32:64]
        out_ref[k, 0:32, 96:128] = grad_numer[32:64]
        out_ref[k, 32:40, 0:64] = grad_row
        out_ref[k, 32:40, 64:128] = grad_row


def attention_call(parts, qkv_weight):
    whole = pl.BlockSpec(memory_space=pltpu.VMEM)
    return pl.pallas_call(
        attention_kernel,
        in_specs=[whole, whole],
        out_specs=[whole, whole],
        out_shape=[
            jax.ShapeDtypeStruct((SUBS, 40, 128), F32),
            jax.ShapeDtypeStruct((WIDTH, 128), F32),
        ],
        compiler_params=pltpu.CompilerParams(vmem_limit_bytes=SMALL_LIMIT),
        name="slice_attention",
    )(parts, qkv_weight)


def backward_kernel(
    counts_ref,
    points_hbm,
    cot_hbm,
    fx_ref,
    gate_ref,
    top_ref,
    scale_ref,
    fb_ref,
    sw_ref,
    w_in_ref,
    w_temp_ref,
    w_out_ref,
    b_out_ref,
    heads_ref,
    grad_qkv_ref,
    result_hbm,
    grad_points_hbm,
    mine_ref,
    theirs_ref,
    result_ref,
    grad_points_ref,
    mixed_ref,
    proj_ref,
    points_ref,
    cot_ref,
    sw_rows_ref,
    token_pad,
    token_cols,
    token_rows,
    grad_tot,
    sems,
):
    get_points = pltpu.make_async_copy(points_hbm, points_ref, sems.at[0])
    get_cot = pltpu.make_async_copy(cot_hbm, cot_ref, sems.at[1])
    put_result = pltpu.make_async_copy(result_ref, result_hbm, sems.at[2])
    put_grad = pltpu.make_async_copy(grad_points_ref, grad_points_hbm, sems.at[3])
    get_points.start()
    get_cot.start()
    sw_rows_ref[...] = jnp.zeros_like(sw_rows_ref)
    for h in range(HEADS):
        group, j = divmod(h, 4)
        sw_rows_ref[group, 32 * j : 32 * j + 32, 64 * j : 64 * j + 64] = sw_ref[h]
    rows = [heads_ref[h, 32:33, :] for h in range(HEADS)]
    square = jnp.concatenate(rows * 16, axis=0).T
    low = lane_ids((64, 128)) < 64
    for group in range(2):
        token_pad[...] = jnp.zeros_like(token_pad)
        for j in range(4):
            h = 4 * group + j
            both = heads_ref[h, 0:32, :]
            turned = pltpu.roll(both, 64, 1)
            lanes = 128 * (j // 2)
            if j % 2 == 0:
                block = jnp.where(low, jnp.concatenate([both, turned], axis=0), 0.0)
            else:
                block = jnp.where(low, 0.0, jnp.concatenate([turned, both], axis=0))
            token_pad[64 * j : 64 * j + 64, lanes : lanes + 128] = block
            grad_tot[64 * h : 64 * h + 64, :] = jnp.broadcast_to(square[0:64, h : h + 1], (64, 128))
        token_cols[group] = token_pad[...].astype(BF16)
        token_rows[group] = token_pad[...].T.astype(BF16)

    inside = inside_row(counts_ref)
    gate = gate_ref[...]
    inv_temper = 1.0 / (0.5 + 1.5 * gate)
    scale_temp = -1.5 * gate * (1.0 - gate) * inv_temper
    b_col = jnp.broadcast_to(b_out_ref[...], (128, D)).T[:, 0:1]
    w_out_t = w_out_ref[...].astype(F32).T.astype(BF16)
    temp_cols = jnp.concatenate([w_temp_ref[...].astype(F32), jnp.zeros((120, D), F32)], axis=0).T
    temp_cols = temp_cols[:, 0:16].astype(BF16)
    temp_rows = []
    slices = []
    for group in range(2):
        fx = fx_ref[128 * group : 128 * group + 128, :]
        raw = tn(sw_rows_ref[group], fx)
        total = nn(token_cols[group], fb_ref[256 * group : 256 * group + 256, :])
        scaled_parts = []
        rounded_parts = []
        for j in range(4):
            h = 4 * group + j
            rows = slice(64 * j, 64 * j + 64)
            logits = raw[rows] * inv_temper[h : h + 1]
            shares = jnp.exp(logits - top_ref[h : h + 1, :]) * scale_ref[h : h + 1, :]
            gt = grad_tot[64 * h : 64 * h + 64, :]
            share_grad = total[rows] + jnp.concatenate([gt] * (ROWS // 128), axis=1)
            inner = jnp.sum(shares * share_grad, axis=0, keepdims=True)
            scaled = shares * (share_grad - inner) * (inside * inv_temper[h : h + 1])
            temp_rows.append(
                jnp.sum(scaled * raw[rows], axis=0, keepdims=True) * scale_temp[h : h + 1]
            )
            scaled_parts.append(scaled.astype(BF16))
            rounded_parts.append((shares * inside).astype(BF16))
        scaled_bf = jnp.concatenate(scaled_parts, axis=0)
        slices.append(nt(fx, scaled_bf))
        proj_ref[128 * group : 128 * group + 128, :] = nn(sw_rows_ref[group], scaled_bf).astype(
            BF16
        )
        pair = nn(token_rows[group], jnp.concatenate(rounded_parts, axis=0)).astype(BF16)
        for j in range(4):
            h = 4 * group + j
            mixed_ref[32 * h : 32 * h + 32, :] = pair[64 * j : 64 * j + 32]
            proj_ref[D + 32 * h : D + 32 * h + 32, :] = pair[64 * j + 32 : 64 * j + 64]
    mixed_ref[D:, :] = jnp.broadcast_to(inside, (16, ROWS)).astype(BF16)
    out = nn(w_out_t, mixed_ref[0:D, :]) + b_col
    result_ref[...] = (out * inside).astype(BF16).T
    proj_ref[2 * D :, :] = jnp.concatenate(
        temp_rows + [jnp.zeros((8, ROWS), F32)], axis=0
    ).astype(BF16)
    grad = nn(w_in_ref[...], proj_ref[0 : 2 * D, :]) + nn(temp_cols, proj_ref[2 * D :, :])
    grad_points_ref[...] = grad.astype(BF16).T
    put_result.start()
    put_grad.start()
    get_points.wait()
    get_cot.wait()
    sum_out = nn(mixed_ref[...], cot_ref[...])
    sum_in = nn(proj_ref[...], points_ref[...])
    turned_in = [sum_in[128 * k : 128 * k + 128, :].T for k in range(4)]
    low = lane_ids((32, 128)) < 64

    def write_first(ref):
        for k in range(3):
            ref[256 * k : 256 * k + 256, :] = turned_in[k]
        for k in range(4):
            group, pair = divmod(k, 2)
            block = slices[group][64 * pair : 64 * pair + 64, 128 * pair : 128 * pair + 128]
            ref[768 + 32 * k : 800 + 32 * k, :] = jnp.where(low, block[0:32], block[32:64])

    def write_second(ref):
        ref[0:256, :] = turned_in[3]
        ref[256:512, :] = sum_out[0:256, 0:128]
        ref[512:768, :] = sum_out[0:256, 128:256]
        ref[768:776, :] = sum_in[512:520, 0:128]
        ref[776:784, :] = sum_in[512:520, 128:256]
        ref[784:792, :] = sum_out[256:264, 0:128]
        ref[792:800, :] = sum_out[256:264, 128:256]
        ref[800:832, :] = grad_qkv_ref[...]
        ref[832:HALF, :] = jnp.zeros((HALF - 832, 128), F32)

    core = device_place()[2]

    @pl.when(core == 0)
    def _():
        write_first(mine_ref)
        write_second(theirs_ref)

    @pl.when(core != 0)
    def _():
        write_first(theirs_ref)
        write_second(mine_ref)

    put_result.wait()
    put_grad.wait()


def backward_call(
    counts, points, cotangent, stash, heads, grad_qkv, w_in, w_temp, slice_weight, w_out, b_out
):
    whole = pl.BlockSpec(memory_space=pltpu.VMEM)
    far = pl.BlockSpec(memory_space=pltpu.HBM)
    block = pl.BlockSpec()
    return pl.pallas_call(
        backward_kernel,
        in_specs=[pl.BlockSpec(memory_space=pltpu.SMEM), far, far] + [whole] * 5
        + [block] * 5
        + [whole, whole],
        out_specs=[far, far, whole, whole],
        out_shape=[
            pltpu.HBM((ROWS, D), BF16),
            pltpu.HBM((ROWS, D), BF16),
            jax.ShapeDtypeStruct((HALF, 128), F32),
            jax.ShapeDtypeStruct((HALF, 128), F32),
        ],
        scratch_shapes=[
            pltpu.VMEM((ROWS, D), BF16),
            pltpu.VMEM((ROWS, D), BF16),
            pltpu.VMEM((D + 16, ROWS), BF16),
            pltpu.VMEM((2 * D + 16, ROWS), BF16),
            pltpu.VMEM((ROWS, D), BF16),
            pltpu.VMEM((ROWS, D), BF16),
            pltpu.VMEM((2, 128, 256), BF16),
            pltpu.VMEM((256, 256), F32),
            pltpu.VMEM((2, 256, 256), BF16),
            pltpu.VMEM((2, 256, 256), BF16),
            pltpu.VMEM((2 * D, 128), F32),
            pltpu.SemaphoreType.DMA((4,)),
        ],
        compiler_params=pltpu.CompilerParams(vmem_limit_bytes=VMEM_LIMIT),
        name="backward",
    )(
        *in_hbm(counts, points, cotangent),
        *stash,
        *in_hbm(slice_weight, w_in, w_temp.T, w_out, b_out.reshape(1, D)),
        heads,
        grad_qkv,
    )


def sum_spread(parts, copies):
    summed = parts[0]
    for k in range(1, parts.shape[0]):
        summed = summed + parts[k]
    return jnp.broadcast_to(summed[None], (copies,) + summed.shape)


def unpack_kernel(
    mine_ref,
    theirs_ref,
    grad_in_ref,
    grad_temp_ref,
    grad_slice_ref,
    grad_out_ref,
    grad_bias_ref,
    grad_qkv_ref,
):
    def unpack(first, second):
        for k in range(3):
            grad_in_ref[:, 128 * k : 128 * k + 128] = first[256 * k : 256 * k + 256, :]
        grad_in_ref[:, 384:512] = second[0:256, :]
        for k in range(4):
            block = first[768 + 32 * k : 800 + 32 * k, :]
            grad_slice_ref[2 * k] = block[:, 0:64]
            grad_slice_ref[2 * k + 1] = pltpu.roll(block, 64, 1)[:, 0:64]
        grad_out_ref[:, 0:128] = second[256:512, :]
        grad_out_ref[:, 128:256] = second[512:768, :]
        for k in range(2):
            rows = second[768 + 8 * k : 776 + 8 * k, :]
            grad_temp_ref[:, 128 * k : 128 * k + 128] = rows
            grad_bias_ref[0:1, 128 * k : 128 * k + 128] = second[784 + 8 * k : 785 + 8 * k, :]
        qkv = second[800:832, :]
        grad_qkv_ref[0] = qkv[:, 0:32]
        grad_qkv_ref[1] = pltpu.roll(qkv, 96, 1)[:, 0:32]
        grad_qkv_ref[2] = pltpu.roll(qkv, 64, 1)[:, 0:32]

    core = device_place()[2]

    @pl.when(core == 0)
    def _():
        unpack(mine_ref, theirs_ref)

    @pl.when(core != 0)
    def _():
        unpack(theirs_ref, mine_ref)


def unpack_call(mine, theirs):
    whole = pl.BlockSpec(memory_space=pltpu.VMEM)
    return pl.pallas_call(
        unpack_kernel,
        in_specs=[whole, whole],
        out_specs=[whole] * 6,
        out_shape=[
            jax.ShapeDtypeStruct((D, 2 * D), F32),
            jax.ShapeDtypeStruct((HEADS, D), F32),
            jax.ShapeDtypeStruct((HEADS, WIDTH, SLICES), F32),
            jax.ShapeDtypeStruct((D, D), F32),
            jax.ShapeDtypeStruct((1, D), F32),
            jax.ShapeDtypeStruct((3, WIDTH, WIDTH), F32),
        ],
        compiler_params=pltpu.CompilerParams(vmem_limit_bytes=SMALL_LIMIT),
        name="unpack",
    )(mine, theirs)


def swap_cores(values):
    return lax.ppermute(values, "core", [(0, 1), (1, 0)])


def spread_over(values, axes):
    return lax.all_to_all(values, axes, 0, 0)


def per_device(points, cotangent, counts, w_in, w_temp, slice_weight, qkv_weight, w_out, b_out):
    packed, *stash = forward_call(counts, points, cotangent, w_in, w_temp, slice_weight, w_out)
    packed = packed + swap_cores(packed)
    parts = sum_spread(spread_over(packed, "sub"), 16)
    parts = spread_over(parts, ("x", "y"))
    heads, grad_qkv = attention_call(parts, qkv_weight)
    heads = spread_over(heads, "sub")
    result, grad_points, mine, theirs = backward_call(
        counts,
        points,
        cotangent,
        stash,
        heads,
        grad_qkv,
        w_in,
        w_temp,
        slice_weight,
        w_out,
        b_out,
    )
    mine = (mine + swap_cores(theirs)).reshape(16, HALF // 16, 128)
    mine = sum_spread(spread_over(mine, ("x", "y")), SUBS)
    mine = sum_spread(spread_over(mine, "sub"), 16)
    mine = spread_over(mine, ("x", "y")).reshape(HALF, 128)
    theirs = swap_cores(mine)
    grad_w_in, grad_w_temp, grad_slice, grad_w_out, grad_bias, grad_qkv = unpack_call(mine, theirs)
    return (
        result,
        grad_points,
        grad_w_in,
        grad_w_temp.T,
        grad_slice,
        grad_w_out,
        grad_bias.reshape(D),
        grad_qkv,
    )


def solution(mesh):
    fine = Mesh(mesh.devices.reshape(4, 4, 2, 8), ("x", "y", "core", "sub"))
    rows = P(("x", "y", "core", "sub"), None)
    return jax.shard_map(
        per_device,
        mesh=fine,
        in_specs=(rows, rows) + (P(),) * 7,
        out_specs=(rows, rows) + (P(),) * 6,
        check_vma=False,
    )
```

```python
import jax
import jax.numpy as jnp
from jax import lax
from jax.experimental import pallas as pl
from jax.experimental.pallas import tpu as pltpu
from jax.sharding import Mesh, PartitionSpec as P

EPSILON = 1e-05
F32 = jnp.float32
BF16 = jnp.bfloat16
HIGH = lax.Precision.HIGHEST

D = 256
HEADS = 8
SLICES = 64
WIDTH = 32
ROWS = 2048
SUBS = 8
HALF = 896
VMEM_LIMIT = 40 * 1024 * 1024
SMALL_LIMIT = 16 * 1024 * 1024


def nn(a, b, precision=None):
    return lax.dot_general(
        a, b, (((1,), (0,)), ((), ())), preferred_element_type=F32, precision=precision
    )


def nt(a, b, precision=None):
    return lax.dot_general(
        a, b, (((1,), (1,)), ((), ())), preferred_element_type=F32, precision=precision
    )


def tn(a, b, precision=None):
    return lax.dot_general(
        a, b, (((0,), (0,)), ((), ())), preferred_element_type=F32, precision=precision
    )


def lane_ids(shape):
    return lax.broadcasted_iota(jnp.int32, shape, 1)


def device_place():
    x, y = lax.axis_index("x"), lax.axis_index("y")
    core, sub = lax.axis_index("core"), lax.axis_index("sub")
    return (x * 4 + y) * 2 + core, sub, core


def live_rows(counts_ref):
    dom, sub, _ = device_place()
    return counts_ref[dom] - sub * ROWS


def in_hbm(*arrays):
    return [pltpu.with_memory_space_constraint(a, pltpu.HBM) for a in arrays]


def inside_row(counts_ref):
    return jnp.where(lane_ids((1, ROWS)) < live_rows(counts_ref), 1.0, 0.0).astype(F32)


def forward_kernel(
    counts_ref,
    points_ref,
    cot_ref,
    w_in_ref,
    w_temp_ref,
    sw_ref,
    w_out_ref,
    packed_ref,
    fx_ref,
    gate_ref,
    top_ref,
    scale_ref,
    fb_ref,
    sw_cols_ref,
    w_all_t,
    sw_pad,
):
    w_all_t[0 : 2 * D, :] = w_in_ref[...].astype(F32).T.astype(BF16)
    w_all_t[2 * D :, :] = jnp.concatenate([w_temp_ref[...], jnp.zeros((8, D), BF16)], axis=0)
    for group in range(2):
        sw_pad[...] = jnp.zeros_like(sw_pad)
        for j in range(4):
            sw_pad[32 * j : 32 * j + 32, 64 * j : 64 * j + 64] = sw_ref[4 * group + j].astype(F32)
        sw_cols_ref[group] = sw_pad[...].T.astype(BF16)
    inside = inside_row(counts_ref)
    projected = nt(w_all_t[...], points_ref[...])
    gate = jax.nn.sigmoid(projected[2 * D : 2 * D + HEADS])
    gate_ref[...] = gate
    inv_temper = 1.0 / (0.5 + 1.5 * gate)
    proj_x = projected[0:D].astype(BF16)
    fx_ref[...] = proj_x
    for h in range(HEADS):
        fb_ref[64 * h + 32 : 64 * h + 64, :] = projected[D + 32 * h : D + 32 * h + 32].astype(BF16)
    back = (nt(w_out_ref[...], cot_ref[...]) * inside).astype(BF16)
    for h in range(HEADS):
        fb_ref[64 * h : 64 * h + 32, :] = back[32 * h : 32 * h + 32]
    sums = []
    folds = []
    for group in range(2):
        raw = nn(sw_cols_ref[group], proj_x[128 * group : 128 * group + 128])
        pieces = []
        for j in range(4):
            h = 4 * group + j
            logits = raw[64 * j : 64 * j + 64] * inv_temper[h : h + 1]
            top = jnp.max(logits, axis=0, keepdims=True)
            ex = jnp.exp(logits - top)
            scale = 1.0 / jnp.sum(ex, axis=0, keepdims=True)
            top_ref[h : h + 1, :] = top
            scale_ref[h : h + 1, :] = scale
            shares = ex * scale
            masked = shares * inside
            folded = masked[:, 0:128]
            for k in range(1, ROWS // 128):
                folded = folded + masked[:, 128 * k : 128 * k + 128]
            folds.append(folded)
            pieces.append(masked.astype(BF16))
        rounded = jnp.concatenate(pieces, axis=0)
        sums.append(nt(rounded, fb_ref[256 * group : 256 * group + 256, :]))
    low = lane_ids((32, 128)) < 64
    totals = nt(jnp.ones((8, 128), F32), jnp.concatenate(folds, axis=0), HIGH)
    for h in range(HEADS):
        group, j = divmod(h, 4)
        lanes = 128 * (j // 2)
        block = sums[group][64 * j : 64 * j + 64, lanes : lanes + 128]
        upper, lower = block[0:32], block[32:64]
        row = totals[:, 128 * (h // 2) : 128 * (h // 2) + 128]
        if j % 2 == 0:
            both = jnp.where(low, upper, pltpu.roll(lower, 64, 1))
        else:
            both = jnp.where(low, pltpu.roll(upper, 64, 1), lower)
            row = pltpu.roll(row, 64, 1)
        packed_ref[h, 0:32, :] = both
        packed_ref[h, 32:40, :] = row


def forward_call(counts, points, cotangent, w_in, w_temp, slice_weight, w_out):
    whole = pl.BlockSpec(memory_space=pltpu.VMEM)
    far = pl.BlockSpec(memory_space=pltpu.HBM)
    block = pl.BlockSpec()
    return pl.pallas_call(
        forward_kernel,
        in_specs=[pl.BlockSpec(memory_space=pltpu.SMEM)] + [block] * 6,
        out_specs=[whole] * 6,
        out_shape=[
            jax.ShapeDtypeStruct((HEADS, 40, 128), F32),
            jax.ShapeDtypeStruct((D, ROWS), BF16),
            jax.ShapeDtypeStruct((HEADS, ROWS), F32),
            jax.ShapeDtypeStruct((HEADS, ROWS), F32),
            jax.ShapeDtypeStruct((HEADS, ROWS), F32),
            jax.ShapeDtypeStruct((2 * D, ROWS), BF16),
        ],
        scratch_shapes=[
            pltpu.VMEM((2, 256, 128), BF16),
            pltpu.VMEM((2 * D + 16, D), BF16),
            pltpu.VMEM((128, 256), F32),
        ],
        compiler_params=pltpu.CompilerParams(vmem_limit_bytes=VMEM_LIMIT),
        name="forward",
    )(*in_hbm(counts, points, cotangent, w_in, w_temp.T, slice_weight, w_out))


def attention_kernel(parts_ref, qkv_ref, out_ref, grad_qkv_ref):
    summed = parts_ref[0]
    for k in range(1, parts_ref.shape[0]):
        summed = summed + parts_ref[k]
    pairs = jnp.concatenate([summed[0:32], pltpu.roll(summed[0:32], 64, 1)], axis=0)
    grad_att = pairs[:, 0:WIDTH]
    numer = pltpu.roll(pairs, 96, 1)[:, 0:WIDTH]
    totals = jnp.concatenate([summed[32:40]] * 16, axis=0).T[0:SLICES, 0:1]
    inv = 1.0 / (totals + EPSILON)
    tokens = numer * inv
    w_q, w_k, w_v = qkv_ref[0], qkv_ref[1], qkv_ref[2]
    scale = WIDTH**-0.5
    query = nn(tokens, w_q, HIGH)
    keys = nn(tokens, w_k, HIGH)
    values = nn(tokens, w_v, HIGH)
    scores = nt(query, keys, HIGH) * scale
    ex = jnp.exp(scores - jnp.max(scores, axis=1, keepdims=True))
    weights = ex / jnp.sum(ex, axis=1, keepdims=True)
    attended = nn(weights, values, HIGH)
    grad_values = tn(weights, grad_att, HIGH)
    grad_weights = nt(grad_att, values, HIGH)
    inner = jnp.sum(weights * grad_weights, axis=1, keepdims=True)
    grad_scores = weights * (grad_weights - inner) * scale
    grad_query = nn(grad_scores, keys, HIGH)
    grad_keys = tn(grad_scores, query, HIGH)
    grad_tokens = (
        nt(grad_query, w_q, HIGH) + nt(grad_keys, w_k, HIGH) + nt(grad_values, w_v, HIGH)
    )
    grad_qkv_ref[...] = jnp.zeros_like(grad_qkv_ref)
    for i, grad in enumerate((grad_query, grad_keys, grad_values)):
        grad_qkv_ref[:, WIDTH * i : WIDTH * i + WIDTH] = tn(tokens, grad, HIGH) * (1.0 / 32)
    grad_numer = grad_tokens * inv
    grad_totals = -jnp.sum(grad_tokens * tokens, axis=1, keepdims=True) * inv
    grad_row = jnp.broadcast_to(grad_totals, (SLICES, 128)).T[0:8]
    for k in range(out_ref.shape[0]):
        out_ref[k, 0:32, 0:32] = attended[0:32]
        out_ref[k, 0:32, 32:64] = grad_numer[0:32]
        out_ref[k, 0:32, 64:96] = attended[32:64]
        out_ref[k, 0:32, 96:128] = grad_numer[32:64]
        out_ref[k, 32:40, 0:64] = grad_row
        out_ref[k, 32:40, 64:128] = grad_row


def attention_call(parts, qkv_weight):
    whole = pl.BlockSpec(memory_space=pltpu.VMEM)
    return pl.pallas_call(
        attention_kernel,
        in_specs=[whole, whole],
        out_specs=[whole, whole],
        out_shape=[
            jax.ShapeDtypeStruct((SUBS, 40, 128), F32),
            jax.ShapeDtypeStruct((WIDTH, 128), F32),
        ],
        compiler_params=pltpu.CompilerParams(vmem_limit_bytes=SMALL_LIMIT),
        name="slice_attention",
    )(parts, qkv_weight)


def backward_kernel(
    counts_ref,
    points_hbm,
    cot_hbm,
    fx_ref,
    gate_ref,
    top_ref,
    scale_ref,
    fb_ref,
    sw_ref,
    w_in_ref,
    w_temp_ref,
    w_out_ref,
    b_out_ref,
    heads_ref,
    grad_qkv_ref,
    result_hbm,
    grad_points_hbm,
    mine_ref,
    theirs_ref,
    result_ref,
    grad_points_ref,
    mixed_ref,
    proj_ref,
    points_ref,
    cot_ref,
    sw_rows_ref,
    token_pad,
    token_cols,
    token_rows,
    grad_tot,
    sems,
):
    get_points = pltpu.make_async_copy(points_hbm, points_ref, sems.at[0])
    get_cot = pltpu.make_async_copy(cot_hbm, cot_ref, sems.at[1])
    put_result = pltpu.make_async_copy(result_ref, result_hbm, sems.at[2])
    put_grad = pltpu.make_async_copy(grad_points_ref, grad_points_hbm, sems.at[3])
    get_points.start()
    get_cot.start()
    sw_rows_ref[...] = jnp.zeros_like(sw_rows_ref)
    for h in range(HEADS):
        group, j = divmod(h, 4)
        sw_rows_ref[group, 32 * j : 32 * j + 32, 64 * j : 64 * j + 64] = sw_ref[h]
    rows = [heads_ref[h, 32:33, :] for h in range(HEADS)]
    square = jnp.concatenate(rows * 16, axis=0).T
    low = lane_ids((64, 128)) < 64
    for group in range(2):
        token_pad[...] = jnp.zeros_like(token_pad)
        for j in range(4):
            h = 4 * group + j
            both = heads_ref[h, 0:32, :]
            turned = pltpu.roll(both, 64, 1)
            lanes = 128 * (j // 2)
            if j % 2 == 0:
                block = jnp.where(low, jnp.concatenate([both, turned], axis=0), 0.0)
            else:
                block = jnp.where(low, 0.0, jnp.concatenate([turned, both], axis=0))
            token_pad[64 * j : 64 * j + 64, lanes : lanes + 128] = block
            grad_tot[64 * h : 64 * h + 64, :] = jnp.broadcast_to(square[0:64, h : h + 1], (64, 128))
        token_cols[group] = token_pad[...].astype(BF16)
        token_rows[group] = token_pad[...].T.astype(BF16)

    inside = inside_row(counts_ref)
    gate = gate_ref[...]
    inv_temper = 1.0 / (0.5 + 1.5 * gate)
    scale_temp = -1.5 * gate * (1.0 - gate) * inv_temper
    b_col = jnp.broadcast_to(b_out_ref[...], (128, D)).T[:, 0:1]
    w_out_t = w_out_ref[...].astype(F32).T.astype(BF16)
    temp_cols = jnp.concatenate([w_temp_ref[...].astype(F32), jnp.zeros((120, D), F32)], axis=0).T
    temp_cols = temp_cols[:, 0:16].astype(BF16)
    temp_rows = []
    slices = []
    for group in range(2):
        fx = fx_ref[128 * group : 128 * group + 128, :]
        raw = tn(sw_rows_ref[group], fx)
        total = nn(token_cols[group], fb_ref[256 * group : 256 * group + 256, :])
        scaled_parts = []
        rounded_parts = []
        for j in range(4):
            h = 4 * group + j
            rows = slice(64 * j, 64 * j + 64)
            logits = raw[rows] * inv_temper[h : h + 1]
            shares = jnp.exp(logits - top_ref[h : h + 1, :]) * scale_ref[h : h + 1, :]
            gt = grad_tot[64 * h : 64 * h + 64, :]
            share_grad = total[rows] + jnp.concatenate([gt] * (ROWS // 128), axis=1)
            inner = jnp.sum(shares * share_grad, axis=0, keepdims=True)
            scaled = shares * (share_grad - inner) * (inside * inv_temper[h : h + 1])
            temp_rows.append(
                jnp.sum(scaled * raw[rows], axis=0, keepdims=True) * scale_temp[h : h + 1]
            )
            scaled_parts.append(scaled.astype(BF16))
            rounded_parts.append((shares * inside).astype(BF16))
        scaled_bf = jnp.concatenate(scaled_parts, axis=0)
        slices.append(nt(fx, scaled_bf))
        proj_ref[128 * group : 128 * group + 128, :] = nn(sw_rows_ref[group], scaled_bf).astype(
            BF16
        )
        pair = nn(token_rows[group], jnp.concatenate(rounded_parts, axis=0)).astype(BF16)
        for j in range(4):
            h = 4 * group + j
            mixed_ref[32 * h : 32 * h + 32, :] = pair[64 * j : 64 * j + 32]
            proj_ref[D + 32 * h : D + 32 * h + 32, :] = pair[64 * j + 32 : 64 * j + 64]
    mixed_ref[D:, :] = jnp.broadcast_to(inside, (16, ROWS)).astype(BF16)
    out = nn(w_out_t, mixed_ref[0:D, :]) + b_col
    result_ref[...] = (out * inside).astype(BF16).T
    proj_ref[2 * D :, :] = jnp.concatenate(
        temp_rows + [jnp.zeros((8, ROWS), F32)], axis=0
    ).astype(BF16)
    grad = nn(w_in_ref[...], proj_ref[0 : 2 * D, :]) + nn(temp_cols, proj_ref[2 * D :, :])
    grad_points_ref[...] = grad.astype(BF16).T
    put_result.start()
    put_grad.start()
    get_points.wait()
    get_cot.wait()
    sum_out = nn(mixed_ref[...], cot_ref[...])
    sum_in = nn(proj_ref[...], points_ref[...])
    turned_in = [sum_in[128 * k : 128 * k + 128, :].T for k in range(4)]
    low = lane_ids((32, 128)) < 64

    def write_first(ref):
        for k in range(3):
            ref[256 * k : 256 * k + 256, :] = turned_in[k]
        for k in range(4):
            group, pair = divmod(k, 2)
            block = slices[group][64 * pair : 64 * pair + 64, 128 * pair : 128 * pair + 128]
            ref[768 + 32 * k : 800 + 32 * k, :] = jnp.where(low, block[0:32], block[32:64])

    def write_second(ref):
        ref[0:256, :] = turned_in[3]
        ref[256:512, :] = sum_out[0:256, 0:128]
        ref[512:768, :] = sum_out[0:256, 128:256]
        ref[768:776, :] = sum_in[512:520, 0:128]
        ref[776:784, :] = sum_in[512:520, 128:256]
        ref[784:792, :] = sum_out[256:264, 0:128]
        ref[792:800, :] = sum_out[256:264, 128:256]
        ref[800:832, :] = grad_qkv_ref[...]
        ref[832:HALF, :] = jnp.zeros((HALF - 832, 128), F32)

    core = device_place()[2]

    @pl.when(core == 0)
    def _():
        write_first(mine_ref)
        write_second(theirs_ref)

    @pl.when(core != 0)
    def _():
        write_first(theirs_ref)
        write_second(mine_ref)

    put_result.wait()
    put_grad.wait()


def backward_call(
    counts, points, cotangent, stash, heads, grad_qkv, w_in, w_temp, slice_weight, w_out, b_out
):
    whole = pl.BlockSpec(memory_space=pltpu.VMEM)
    far = pl.BlockSpec(memory_space=pltpu.HBM)
    block = pl.BlockSpec()
    return pl.pallas_call(
        backward_kernel,
        in_specs=[pl.BlockSpec(memory_space=pltpu.SMEM), far, far] + [whole] * 5
        + [block] * 5
        + [whole, whole],
        out_specs=[far, far, whole, whole],
        out_shape=[
            pltpu.HBM((ROWS, D), BF16),
            pltpu.HBM((ROWS, D), BF16),
            jax.ShapeDtypeStruct((HALF, 128), F32),
            jax.ShapeDtypeStruct((HALF, 128), F32),
        ],
        scratch_shapes=[
            pltpu.VMEM((ROWS, D), BF16),
            pltpu.VMEM((ROWS, D), BF16),
            pltpu.VMEM((D + 16, ROWS), BF16),
            pltpu.VMEM((2 * D + 16, ROWS), BF16),
            pltpu.VMEM((ROWS, D), BF16),
            pltpu.VMEM((ROWS, D), BF16),
            pltpu.VMEM((2, 128, 256), BF16),
            pltpu.VMEM((256, 256), F32),
            pltpu.VMEM((2, 256, 256), BF16),
            pltpu.VMEM((2, 256, 256), BF16),
            pltpu.VMEM((2 * D, 128), F32),
            pltpu.SemaphoreType.DMA((4,)),
        ],
        compiler_params=pltpu.CompilerParams(vmem_limit_bytes=VMEM_LIMIT),
        name="backward",
    )(
        *in_hbm(counts, points, cotangent),
        *stash,
        *in_hbm(slice_weight, w_in, w_temp.T, w_out, b_out.reshape(1, D)),
        heads,
        grad_qkv,
    )


def sum_parts(parts):
    summed = parts[0]
    for k in range(1, parts.shape[0]):
        summed = summed + parts[k]
    return summed


def spread(summed, copies):
    return jnp.broadcast_to(summed[None], (copies,) + summed.shape)


def sum_spread(parts, copies):
    return spread(sum_parts(parts), copies)


def unpack_kernel(
    mine_ref,
    theirs_ref,
    grad_in_hbm,
    grad_temp_ref,
    grad_slice_ref,
    grad_out_hbm,
    grad_bias_ref,
    grad_qkv_ref,
    sems,
):
    def big_copies(first, second):
        blocks = [(first, k, grad_in_hbm, k) for k in range(3)]
        blocks += [(second, 0, grad_in_hbm, 3)]
        blocks += [(second, 1 + k, grad_out_hbm, k) for k in range(2)]
        return [
            pltpu.make_async_copy(
                ref.at[pl.ds(256 * k, 256)], out.at[:, pl.ds(128 * at, 128)], sems.at[i]
            )
            for i, (ref, k, out, at) in enumerate(blocks)
        ]

    def unpack(first, second):
        copies = big_copies(first, second)
        for copy in copies:
            copy.start()
        for k in range(4):
            block = first[768 + 32 * k : 800 + 32 * k, :]
            grad_slice_ref[2 * k] = block[:, 0:64]
            grad_slice_ref[2 * k + 1] = pltpu.roll(block, 64, 1)[:, 0:64]
        for k in range(2):
            rows = second[768 + 8 * k : 776 + 8 * k, :]
            grad_temp_ref[:, 128 * k : 128 * k + 128] = rows
            grad_bias_ref[0:1, 128 * k : 128 * k + 128] = second[784 + 8 * k : 785 + 8 * k, :]
        qkv = second[800:832, :]
        grad_qkv_ref[0] = qkv[:, 0:32]
        grad_qkv_ref[1] = pltpu.roll(qkv, 96, 1)[:, 0:32]
        grad_qkv_ref[2] = pltpu.roll(qkv, 64, 1)[:, 0:32]
        for copy in copies:
            copy.wait()

    core = device_place()[2]

    @pl.when(core == 0)
    def _():
        unpack(mine_ref, theirs_ref)

    @pl.when(core != 0)
    def _():
        unpack(theirs_ref, mine_ref)


def unpack_call(mine, theirs):
    whole = pl.BlockSpec(memory_space=pltpu.VMEM)
    far = pl.BlockSpec(memory_space=pltpu.HBM)
    return pl.pallas_call(
        unpack_kernel,
        in_specs=[whole, whole],
        out_specs=[far, whole, whole, far, whole, whole],
        out_shape=[
            pltpu.HBM((D, 2 * D), F32),
            jax.ShapeDtypeStruct((HEADS, D), F32),
            jax.ShapeDtypeStruct((HEADS, WIDTH, SLICES), F32),
            pltpu.HBM((D, D), F32),
            jax.ShapeDtypeStruct((1, D), F32),
            jax.ShapeDtypeStruct((3, WIDTH, WIDTH), F32),
        ],
        scratch_shapes=[pltpu.SemaphoreType.DMA((6,))],
        compiler_params=pltpu.CompilerParams(vmem_limit_bytes=SMALL_LIMIT),
        name="unpack",
    )(mine, theirs)


def swap_cores(values):
    return lax.ppermute(values, "core", [(0, 1), (1, 0)])


def spread_over(values, axes):
    return lax.all_to_all(values, axes, 0, 0)


def per_device(points, cotangent, counts, w_in, w_temp, slice_weight, qkv_weight, w_out, b_out):
    packed, *stash = forward_call(counts, points, cotangent, w_in, w_temp, slice_weight, w_out)
    summed = sum_parts(spread_over(packed, "sub"))
    parts = spread_over(spread(summed + swap_cores(summed), 16), ("x", "y"))
    heads, grad_qkv = attention_call(parts, qkv_weight)
    heads = spread_over(heads, "sub")
    result, grad_points, mine, theirs = backward_call(
        counts,
        points,
        cotangent,
        stash,
        heads,
        grad_qkv,
        w_in,
        w_temp,
        slice_weight,
        w_out,
        b_out,
    )
    mine = (mine + swap_cores(theirs)).reshape(16, HALF // 16, 128)
    mine = sum_spread(spread_over(mine, ("x", "y")), SUBS)
    mine = sum_spread(spread_over(mine, "sub"), 16)
    mine = spread_over(mine, ("x", "y")).reshape(HALF, 128)
    theirs = swap_cores(mine)
    grad_w_in, grad_w_temp, grad_slice, grad_w_out, grad_bias, grad_qkv = unpack_call(mine, theirs)
    return (
        result,
        grad_points,
        grad_w_in,
        grad_w_temp.T,
        grad_slice,
        grad_w_out,
        grad_bias.reshape(D),
        grad_qkv,
    )


def solution(mesh):
    fine = Mesh(mesh.devices.reshape(4, 4, 2, 8), ("x", "y", "core", "sub"))
    rows = P(("x", "y", "core", "sub"), None)
    return jax.shard_map(
        per_device,
        mesh=fine,
        in_specs=(rows, rows) + (P(),) * 7,
        out_specs=(rows, rows) + (P(),) * 6,
        check_vma=False,
    )
```

```python
import jax
import jax.numpy as jnp
from jax import lax
from jax.experimental import pallas as pl
from jax.experimental.pallas import tpu as pltpu
from jax.sharding import Mesh, PartitionSpec as P

EPSILON = 1e-05
F32 = jnp.float32
BF16 = jnp.bfloat16
HIGH = lax.Precision.HIGHEST

D = 256
HEADS = 8
SLICES = 64
WIDTH = 32
ROWS = 2048
SUBS = 8
HALF = 896
VMEM_LIMIT = 40 * 1024 * 1024
SMALL_LIMIT = 16 * 1024 * 1024


def nn(a, b, precision=None):
    return lax.dot_general(
        a, b, (((1,), (0,)), ((), ())), preferred_element_type=F32, precision=precision
    )


def nt(a, b, precision=None):
    return lax.dot_general(
        a, b, (((1,), (1,)), ((), ())), preferred_element_type=F32, precision=precision
    )


def tn(a, b, precision=None):
    return lax.dot_general(
        a, b, (((0,), (0,)), ((), ())), preferred_element_type=F32, precision=precision
    )


def lane_ids(shape):
    return lax.broadcasted_iota(jnp.int32, shape, 1)


def device_place():
    x, y = lax.axis_index("x"), lax.axis_index("y")
    core, sub = lax.axis_index("core"), lax.axis_index("sub")
    return (x * 4 + y) * 2 + core, sub, core


def live_rows(counts_ref):
    dom, sub, _ = device_place()
    return counts_ref[dom] - sub * ROWS


def in_hbm(*arrays):
    return [pltpu.with_memory_space_constraint(a, pltpu.HBM) for a in arrays]


def inside_row(counts_ref):
    return jnp.where(lane_ids((1, ROWS)) < live_rows(counts_ref), 1.0, 0.0).astype(F32)


def forward_kernel(
    counts_ref,
    points_ref,
    cot_ref,
    w_in_ref,
    w_temp_ref,
    sw_ref,
    w_out_ref,
    packed_ref,
    fx_ref,
    gate_ref,
    top_ref,
    scale_ref,
    fb_ref,
    sw_cols_ref,
    w_all_t,
    sw_pad,
):
    w_all_t[0 : 2 * D, :] = w_in_ref[...].astype(F32).T.astype(BF16)
    w_all_t[2 * D :, :] = jnp.concatenate([w_temp_ref[...], jnp.zeros((8, D), BF16)], axis=0)
    for group in range(2):
        sw_pad[...] = jnp.zeros_like(sw_pad)
        for j in range(4):
            sw_pad[32 * j : 32 * j + 32, 64 * j : 64 * j + 64] = sw_ref[4 * group + j].astype(F32)
        sw_cols_ref[group] = sw_pad[...].T.astype(BF16)
    inside = inside_row(counts_ref)
    projected = nt(w_all_t[...], points_ref[...])
    gate = jax.nn.sigmoid(projected[2 * D : 2 * D + HEADS])
    gate_ref[...] = gate
    inv_temper = 1.0 / (0.5 + 1.5 * gate)
    proj_x = projected[0:D].astype(BF16)
    fx_ref[...] = proj_x
    for h in range(HEADS):
        fb_ref[64 * h + 32 : 64 * h + 64, :] = projected[D + 32 * h : D + 32 * h + 32].astype(BF16)
    back = (nt(w_out_ref[...], cot_ref[...]) * inside).astype(BF16)
    for h in range(HEADS):
        fb_ref[64 * h : 64 * h + 32, :] = back[32 * h : 32 * h + 32]
    sums = []
    folds = []
    for group in range(2):
        raw = nn(sw_cols_ref[group], proj_x[128 * group : 128 * group + 128])
        pieces = []
        for j in range(4):
            h = 4 * group + j
            logits = raw[64 * j : 64 * j + 64] * inv_temper[h : h + 1]
            top = jnp.max(logits, axis=0, keepdims=True)
            ex = jnp.exp(logits - top)
            scale = 1.0 / jnp.sum(ex, axis=0, keepdims=True)
            top_ref[h : h + 1, :] = top
            scale_ref[h : h + 1, :] = scale
            shares = ex * scale
            masked = shares * inside
            folded = masked[:, 0:128]
            for k in range(1, ROWS // 128):
                folded = folded + masked[:, 128 * k : 128 * k + 128]
            folds.append(folded)
            pieces.append(masked.astype(BF16))
        rounded = jnp.concatenate(pieces, axis=0)
        sums.append(nt(rounded, fb_ref[256 * group : 256 * group + 256, :]))
    low = lane_ids((32, 128)) < 64
    totals = nt(jnp.ones((8, 128), F32), jnp.concatenate(folds, axis=0), HIGH)
    for h in range(HEADS):
        group, j = divmod(h, 4)
        lanes = 128 * (j // 2)
        block = sums[group][64 * j : 64 * j + 64, lanes : lanes + 128]
        upper, lower = block[0:32], block[32:64]
        row = totals[:, 128 * (h // 2) : 128 * (h // 2) + 128]
        if j % 2 == 0:
            both = jnp.where(low, upper, pltpu.roll(lower, 64, 1))
        else:
            both = jnp.where(low, pltpu.roll(upper, 64, 1), lower)
            row = pltpu.roll(row, 64, 1)
        packed_ref[h, 0:32, :] = both
        packed_ref[h, 32:40, :] = row


def forward_call(counts, points, cotangent, w_in, w_temp, slice_weight, w_out):
    whole = pl.BlockSpec(memory_space=pltpu.VMEM)
    far = pl.BlockSpec(memory_space=pltpu.HBM)
    block = pl.BlockSpec()
    return pl.pallas_call(
        forward_kernel,
        in_specs=[pl.BlockSpec(memory_space=pltpu.SMEM)] + [block] * 6,
        out_specs=[whole] * 6,
        out_shape=[
            jax.ShapeDtypeStruct((HEADS, 40, 128), F32),
            jax.ShapeDtypeStruct((D, ROWS), BF16),
            jax.ShapeDtypeStruct((HEADS, ROWS), F32),
            jax.ShapeDtypeStruct((HEADS, ROWS), F32),
            jax.ShapeDtypeStruct((HEADS, ROWS), F32),
            jax.ShapeDtypeStruct((2 * D, ROWS), BF16),
        ],
        scratch_shapes=[
            pltpu.VMEM((2, 256, 128), BF16),
            pltpu.VMEM((2 * D + 16, D), BF16),
            pltpu.VMEM((128, 256), F32),
        ],
        compiler_params=pltpu.CompilerParams(vmem_limit_bytes=VMEM_LIMIT),
        name="forward",
    )(*in_hbm(counts, points, cotangent, w_in, w_temp.T, slice_weight, w_out))


def attention_kernel(parts_ref, qkv_ref, out_ref, grad_qkv_ref):
    summed = parts_ref[0]
    for k in range(1, parts_ref.shape[0]):
        summed = summed + parts_ref[k]
    pairs = jnp.concatenate([summed[0:32], pltpu.roll(summed[0:32], 64, 1)], axis=0)
    grad_att = pairs[:, 0:WIDTH]
    numer = pltpu.roll(pairs, 96, 1)[:, 0:WIDTH]
    totals = jnp.concatenate([summed[32:40]] * 16, axis=0).T[0:SLICES, 0:1]
    inv = 1.0 / (totals + EPSILON)
    tokens = numer * inv
    w_q, w_k, w_v = qkv_ref[0], qkv_ref[1], qkv_ref[2]
    scale = WIDTH**-0.5
    query = nn(tokens, w_q, HIGH)
    keys = nn(tokens, w_k, HIGH)
    values = nn(tokens, w_v, HIGH)
    scores = nt(query, keys, HIGH) * scale
    ex = jnp.exp(scores - jnp.max(scores, axis=1, keepdims=True))
    weights = ex / jnp.sum(ex, axis=1, keepdims=True)
    attended = nn(weights, values, HIGH)
    grad_values = tn(weights, grad_att, HIGH)
    grad_weights = nt(grad_att, values, HIGH)
    inner = jnp.sum(weights * grad_weights, axis=1, keepdims=True)
    grad_scores = weights * (grad_weights - inner) * scale
    grad_query = nn(grad_scores, keys, HIGH)
    grad_keys = tn(grad_scores, query, HIGH)
    grads = jnp.concatenate([grad_query, grad_keys, grad_values], axis=1)
    grad_tokens = nt(grads, jnp.concatenate([w_q, w_k, w_v], axis=1), HIGH)
    grad_qkv_ref[...] = jnp.zeros_like(grad_qkv_ref)
    grad_qkv_ref[:, 0 : 3 * WIDTH] = tn(tokens, grads, HIGH) * (1.0 / 32)
    grad_numer = grad_tokens * inv
    grad_totals = -jnp.sum(grad_tokens * tokens, axis=1, keepdims=True) * inv
    grad_row = jnp.broadcast_to(grad_totals, (SLICES, 128)).T[0:8]
    block = jnp.concatenate(
        [attended[0:32], grad_numer[0:32], attended[32:64], grad_numer[32:64]], axis=1
    )
    rows = jnp.concatenate([grad_row, grad_row], axis=1)
    for k in range(out_ref.shape[0]):
        out_ref[k, 0:32, :] = block
        out_ref[k, 32:40, :] = rows


def attention_call(parts, qkv_weight):
    whole = pl.BlockSpec(memory_space=pltpu.VMEM)
    return pl.pallas_call(
        attention_kernel,
        in_specs=[whole, whole],
        out_specs=[whole, whole],
        out_shape=[
            jax.ShapeDtypeStruct((SUBS, 40, 128), F32),
            jax.ShapeDtypeStruct((WIDTH, 128), F32),
        ],
        compiler_params=pltpu.CompilerParams(vmem_limit_bytes=SMALL_LIMIT),
        name="slice_attention",
    )(parts, qkv_weight)


def backward_kernel(
    counts_ref,
    points_hbm,
    cot_hbm,
    fx_ref,
    gate_ref,
    top_ref,
    scale_ref,
    fb_ref,
    sw_ref,
    w_in_ref,
    w_temp_ref,
    w_out_ref,
    b_out_ref,
    heads_ref,
    grad_qkv_ref,
    result_hbm,
    grad_points_hbm,
    mine_ref,
    theirs_ref,
    result_ref,
    grad_points_ref,
    mixed_ref,
    proj_ref,
    points_ref,
    cot_ref,
    sw_rows_ref,
    token_pad,
    token_cols,
    token_rows,
    grad_tot,
    sems,
):
    get_points = pltpu.make_async_copy(points_hbm, points_ref, sems.at[0])
    get_cot = pltpu.make_async_copy(cot_hbm, cot_ref, sems.at[1])
    put_result = pltpu.make_async_copy(result_ref, result_hbm, sems.at[2])
    put_grad = pltpu.make_async_copy(grad_points_ref, grad_points_hbm, sems.at[3])
    get_points.start()
    get_cot.start()
    sw_rows_ref[...] = jnp.zeros_like(sw_rows_ref)
    for h in range(HEADS):
        group, j = divmod(h, 4)
        sw_rows_ref[group, 32 * j : 32 * j + 32, 64 * j : 64 * j + 64] = sw_ref[h]
    rows = [heads_ref[h, 32:33, :] for h in range(HEADS)]
    square = jnp.concatenate(rows * 16, axis=0).T
    low = lane_ids((64, 128)) < 64
    for group in range(2):
        token_pad[...] = jnp.zeros_like(token_pad)
        for j in range(4):
            h = 4 * group + j
            both = heads_ref[h, 0:32, :]
            turned = pltpu.roll(both, 64, 1)
            lanes = 128 * (j // 2)
            if j % 2 == 0:
                block = jnp.where(low, jnp.concatenate([both, turned], axis=0), 0.0)
            else:
                block = jnp.where(low, 0.0, jnp.concatenate([turned, both], axis=0))
            token_pad[64 * j : 64 * j + 64, lanes : lanes + 128] = block
            grad_tot[64 * h : 64 * h + 64, :] = jnp.broadcast_to(square[0:64, h : h + 1], (64, 128))
        token_cols[group] = token_pad[...].astype(BF16)
        token_rows[group] = token_pad[...].T.astype(BF16)

    inside = inside_row(counts_ref)
    gate = gate_ref[...]
    inv_temper = 1.0 / (0.5 + 1.5 * gate)
    scale_temp = -1.5 * gate * (1.0 - gate) * inv_temper
    b_col = jnp.broadcast_to(b_out_ref[...], (128, D)).T[:, 0:1]
    w_out_t = w_out_ref[...].astype(F32).T.astype(BF16)
    temp_cols = jnp.concatenate([w_temp_ref[...].astype(F32), jnp.zeros((120, D), F32)], axis=0).T
    temp_cols = temp_cols[:, 0:16].astype(BF16)
    temp_rows = []
    slices = []
    for group in range(2):
        fx = fx_ref[128 * group : 128 * group + 128, :]
        raw = tn(sw_rows_ref[group], fx)
        total = nn(token_cols[group], fb_ref[256 * group : 256 * group + 256, :])
        scaled_parts = []
        rounded_parts = []
        for j in range(4):
            h = 4 * group + j
            rows = slice(64 * j, 64 * j + 64)
            logits = raw[rows] * inv_temper[h : h + 1]
            shares = jnp.exp(logits - top_ref[h : h + 1, :]) * scale_ref[h : h + 1, :]
            gt = grad_tot[64 * h : 64 * h + 64, :]
            share_grad = total[rows] + jnp.concatenate([gt] * (ROWS // 128), axis=1)
            inner = jnp.sum(shares * share_grad, axis=0, keepdims=True)
            scaled = shares * (share_grad - inner) * (inside * inv_temper[h : h + 1])
            temp_rows.append(
                jnp.sum(scaled * raw[rows], axis=0, keepdims=True) * scale_temp[h : h + 1]
            )
            scaled_parts.append(scaled.astype(BF16))
            rounded_parts.append((shares * inside).astype(BF16))
        scaled_bf = jnp.concatenate(scaled_parts, axis=0)
        slices.append(nt(fx, scaled_bf))
        proj_ref[128 * group : 128 * group + 128, :] = nn(sw_rows_ref[group], scaled_bf).astype(
            BF16
        )
        pair = nn(token_rows[group], jnp.concatenate(rounded_parts, axis=0)).astype(BF16)
        for j in range(4):
            h = 4 * group + j
            mixed_ref[32 * h : 32 * h + 32, :] = pair[64 * j : 64 * j + 32]
            proj_ref[D + 32 * h : D + 32 * h + 32, :] = pair[64 * j + 32 : 64 * j + 64]
    mixed_ref[D:, :] = jnp.broadcast_to(inside, (16, ROWS)).astype(BF16)
    out = nn(w_out_t, mixed_ref[0:D, :]) + b_col
    result_ref[...] = (out * inside).astype(BF16).T
    proj_ref[2 * D :, :] = jnp.concatenate(
        temp_rows + [jnp.zeros((8, ROWS), F32)], axis=0
    ).astype(BF16)
    grad = nn(w_in_ref[...], proj_ref[0 : 2 * D, :]) + nn(temp_cols, proj_ref[2 * D :, :])
    grad_points_ref[...] = grad.astype(BF16).T
    put_result.start()
    put_grad.start()
    get_points.wait()
    get_cot.wait()
    sum_out = nn(mixed_ref[...], cot_ref[...])
    sum_in = nn(proj_ref[...], points_ref[...])
    turned_in = [sum_in[128 * k : 128 * k + 128, :].T for k in range(4)]
    low = lane_ids((32, 128)) < 64

    def write_first(ref):
        for k in range(3):
            ref[256 * k : 256 * k + 256, :] = turned_in[k]
        for k in range(4):
            group, pair = divmod(k, 2)
            block = slices[group][64 * pair : 64 * pair + 64, 128 * pair : 128 * pair + 128]
            ref[768 + 32 * k : 800 + 32 * k, :] = jnp.where(low, block[0:32], block[32:64])

    def write_second(ref):
        ref[0:256, :] = turned_in[3]
        ref[256:512, :] = sum_out[0:256, 0:128]
        ref[512:768, :] = sum_out[0:256, 128:256]
        ref[768:776, :] = sum_in[512:520, 0:128]
        ref[776:784, :] = sum_in[512:520, 128:256]
        ref[784:792, :] = sum_out[256:264, 0:128]
        ref[792:800, :] = sum_out[256:264, 128:256]
        ref[800:832, :] = grad_qkv_ref[...]
        ref[832:HALF, :] = jnp.zeros((HALF - 832, 128), F32)

    core = device_place()[2]

    @pl.when(core == 0)
    def _():
        write_first(mine_ref)
        write_second(theirs_ref)

    @pl.when(core != 0)
    def _():
        write_first(theirs_ref)
        write_second(mine_ref)

    put_result.wait()
    put_grad.wait()


def backward_call(
    counts, points, cotangent, stash, heads, grad_qkv, w_in, w_temp, slice_weight, w_out, b_out
):
    whole = pl.BlockSpec(memory_space=pltpu.VMEM)
    far = pl.BlockSpec(memory_space=pltpu.HBM)
    block = pl.BlockSpec()
    return pl.pallas_call(
        backward_kernel,
        in_specs=[pl.BlockSpec(memory_space=pltpu.SMEM), far, far] + [whole] * 5
        + [block] * 5
        + [whole, whole],
        out_specs=[far, far, whole, whole],
        out_shape=[
            pltpu.HBM((ROWS, D), BF16),
            pltpu.HBM((ROWS, D), BF16),
            jax.ShapeDtypeStruct((HALF, 128), F32),
            jax.ShapeDtypeStruct((HALF, 128), F32),
        ],
        scratch_shapes=[
            pltpu.VMEM((ROWS, D), BF16),
            pltpu.VMEM((ROWS, D), BF16),
            pltpu.VMEM((D + 16, ROWS), BF16),
            pltpu.VMEM((2 * D + 16, ROWS), BF16),
            pltpu.VMEM((ROWS, D), BF16),
            pltpu.VMEM((ROWS, D), BF16),
            pltpu.VMEM((2, 128, 256), BF16),
            pltpu.VMEM((256, 256), F32),
            pltpu.VMEM((2, 256, 256), BF16),
            pltpu.VMEM((2, 256, 256), BF16),
            pltpu.VMEM((2 * D, 128), F32),
            pltpu.SemaphoreType.DMA((4,)),
        ],
        compiler_params=pltpu.CompilerParams(vmem_limit_bytes=VMEM_LIMIT),
        name="backward",
    )(
        *in_hbm(counts, points, cotangent),
        *stash,
        *in_hbm(slice_weight, w_in, w_temp.T, w_out, b_out.reshape(1, D)),
        heads,
        grad_qkv,
    )


def sum_spread(parts, copies):
    summed = parts[0]
    for k in range(1, parts.shape[0]):
        summed = summed + parts[k]
    return jnp.broadcast_to(summed[None], (copies,) + summed.shape)


def unpack_kernel(
    mine_ref,
    theirs_ref,
    grad_in_ref,
    grad_temp_ref,
    grad_slice_ref,
    grad_out_ref,
    grad_bias_ref,
    grad_qkv_ref,
):
    def unpack(first, second):
        for k in range(3):
            grad_in_ref[:, 128 * k : 128 * k + 128] = first[256 * k : 256 * k + 256, :]
        grad_in_ref[:, 384:512] = second[0:256, :]
        for k in range(4):
            block = first[768 + 32 * k : 800 + 32 * k, :]
            grad_slice_ref[2 * k] = block[:, 0:64]
            grad_slice_ref[2 * k + 1] = pltpu.roll(block, 64, 1)[:, 0:64]
        grad_out_ref[:, 0:128] = second[256:512, :]
        grad_out_ref[:, 128:256] = second[512:768, :]
        for k in range(2):
            rows = second[768 + 8 * k : 776 + 8 * k, :]
            grad_temp_ref[:, 128 * k : 128 * k + 128] = rows
            grad_bias_ref[0:1, 128 * k : 128 * k + 128] = second[784 + 8 * k : 785 + 8 * k, :]
        qkv = second[800:832, :]
        grad_qkv_ref[0] = qkv[:, 0:32]
        grad_qkv_ref[1] = pltpu.roll(qkv, 96, 1)[:, 0:32]
        grad_qkv_ref[2] = pltpu.roll(qkv, 64, 1)[:, 0:32]

    core = device_place()[2]

    @pl.when(core == 0)
    def _():
        unpack(mine_ref, theirs_ref)

    @pl.when(core != 0)
    def _():
        unpack(theirs_ref, mine_ref)


def unpack_call(mine, theirs):
    whole = pl.BlockSpec(memory_space=pltpu.VMEM)
    return pl.pallas_call(
        unpack_kernel,
        in_specs=[whole, whole],
        out_specs=[whole] * 6,
        out_shape=[
            jax.ShapeDtypeStruct((D, 2 * D), F32),
            jax.ShapeDtypeStruct((HEADS, D), F32),
            jax.ShapeDtypeStruct((HEADS, WIDTH, SLICES), F32),
            jax.ShapeDtypeStruct((D, D), F32),
            jax.ShapeDtypeStruct((1, D), F32),
            jax.ShapeDtypeStruct((3, WIDTH, WIDTH), F32),
        ],
        compiler_params=pltpu.CompilerParams(vmem_limit_bytes=SMALL_LIMIT),
        name="unpack",
    )(mine, theirs)


def swap_cores(values):
    return lax.ppermute(values, "core", [(0, 1), (1, 0)])


def spread_over(values, axes):
    return lax.all_to_all(values, axes, 0, 0)


def per_device(points, cotangent, counts, w_in, w_temp, slice_weight, qkv_weight, w_out, b_out):
    packed, *stash = forward_call(counts, points, cotangent, w_in, w_temp, slice_weight, w_out)
    packed = packed + swap_cores(packed)
    parts = sum_spread(spread_over(packed, "sub"), 16)
    parts = spread_over(parts, ("x", "y"))
    heads, grad_qkv = attention_call(parts, qkv_weight)
    heads = spread_over(heads, "sub")
    result, grad_points, mine, theirs = backward_call(
        counts,
        points,
        cotangent,
        stash,
        heads,
        grad_qkv,
        w_in,
        w_temp,
        slice_weight,
        w_out,
        b_out,
    )
    mine = (mine + swap_cores(theirs)).reshape(16, HALF // 16, 128)
    mine = sum_spread(spread_over(mine, ("x", "y")), SUBS)
    mine = sum_spread(spread_over(mine, "sub"), 16)
    mine = spread_over(mine, ("x", "y")).reshape(HALF, 128)
    theirs = swap_cores(mine)
    grad_w_in, grad_w_temp, grad_slice, grad_w_out, grad_bias, grad_qkv = unpack_call(mine, theirs)
    return (
        result,
        grad_points,
        grad_w_in,
        grad_w_temp.T,
        grad_slice,
        grad_w_out,
        grad_bias.reshape(D),
        grad_qkv,
    )


def solution(mesh):
    fine = Mesh(mesh.devices.reshape(4, 4, 2, 8), ("x", "y", "core", "sub"))
    rows = P(("x", "y", "core", "sub"), None)
    return jax.shard_map(
        per_device,
        mesh=fine,
        in_specs=(rows, rows) + (P(),) * 7,
        out_specs=(rows, rows) + (P(),) * 6,
        check_vma=False,
    )
```
